32 devices in a mesh: rows: 16 (over z, y, core), cols: 2 (over x).
Axes of the slice: x: 2, y: 2, z: 4, core: 2. Of those that a mesh axis runs over, the one named last changes fastest.
Arguments:
- vectors: float32 [128, 32768], P(None, ('rows', 'cols')), may hold values from -80 to 80
- offsets: int32 [16, 32768], P(None, ('rows', 'cols')), may hold values from -256 to 256, as said below
- counts: int32 [32768], P(('rows', 'cols')), may hold values from 8 to 16
- labels: int32 [2, 32768], P(None, ('rows', 'cols')), may hold values from 0 to 1
- cosines: float32 [16, 32768], P(None, ('rows', 'cols')), may hold values from -1 to 1
- distances: float32 [16, 32768], P(None, ('rows', 'cols')), may hold values from 1 to 3
Outputs:
- basis: float32 [128, 32768], P('cols', 'rows')
The draws below stay inside these ranges and needn't reach their ends.
Inputs may be any that keep to these rules, and one draw needn't show every extreme that they name: `offsets`: each offset is nonzero and at most 256 in magnitude; both -256 and 256 occur. Offsets follow a lattice: small in-row steps, steps near half of 256, and steps near 256.
All inputs are finite; a program needn't handle non-finite values.
Results may differ from the reference program's by a relative error of at most 0.00012.
Values sent between devices are 32-bit elements; how exact they have to be, the bound alone decides.
A program may use at most 64 MiB of HBM per device.

```python
import math
import jax
import jax.numpy as jnp
from jax import lax

BLOCK = 64
SLOTS = 16
REACH = 256
NV = 128
ATOMS = 32768
STEPS = 1


def geometry(key):
    base_key = jax.random.fold_in(key, 11)
    first_key, second_key = jax.random.split(base_key, 2)
    cosine_part = jax.random.uniform(first_key, (SLOTS, ATOMS), jnp.float32, -1.0, 1.0)
    spread = jax.random.uniform(second_key, (SLOTS, ATOMS), jnp.float32, 0.0, 0.6)
    length = 1.0 + 1.36 * cosine_part * cosine_part + spread
    return (cosine_part, length)


def draw_cosines(key, part):
    return geometry(key)[0].astype(jnp.float32)


def draw_distances(key, part):
    return geometry(key)[1].astype(jnp.float32)


def draw_offsets(key, part):
    base_key = jax.random.fold_in(key, 23)
    keys = jax.random.split(base_key, 6)
    kind = jax.random.randint(keys[0], (SLOTS, ATOMS), 0, 3)
    signs = jax.random.randint(keys[1], (SLOTS, ATOMS), 0, 2) * 2 - 1
    near_step = 1 + jax.random.randint(keys[2], (SLOTS, ATOMS), 0, 2)
    middle_step = REACH // 2 + jax.random.randint(keys[3], (SLOTS, ATOMS), -2, 3)
    far_step = REACH - jax.random.randint(keys[4], (SLOTS, ATOMS), 0, 3)
    magnitude = jnp.where(kind == 0, near_step, jnp.where(kind == 1, middle_step, far_step))
    magnitude = jnp.clip(magnitude, 1, REACH)
    spots = jax.random.randint(keys[5], (2,), 0, ATOMS)
    shifted = magnitude * signs
    shifted = shifted.at[0, spots[0]].set(REACH)
    shifted = shifted.at[1, spots[1]].set(-REACH)
    return shifted.astype(jnp.int32)


def draw_vectors(key, part):
    base_key = jax.random.fold_in(key, 31)
    keys = jax.random.split(base_key, 3)
    position = jnp.arange(ATOMS, dtype=jnp.float32) / ATOMS
    row_scale = jnp.exp(jax.random.uniform(keys[0], (1, ATOMS), jnp.float32, math.log(0.3), math.log(3.0)))
    col_scale = jnp.exp(jax.random.uniform(keys[1], (NV, 1), jnp.float32, math.log(0.3), math.log(3.0)))
    core = jnp.clip(jax.random.normal(keys[2], (NV, ATOMS), jnp.float32), -4.0, 4.0)
    trend = 1.0 + 2.0 * position[None, :]
    result = core * row_scale * trend * col_scale / 1.5
    return result.astype(jnp.float32)


def with_ends(drawn, key, low, top_value):
    longest = drawn.shape.index(max(drawn.shape))
    spots = []
    for shift in (0, 1):
        where = [jax.random.randint(jax.random.fold_in(key, axis), (), 0, length) for axis, length in enumerate(drawn.shape)]
        where[longest] = (where[longest] + shift) % drawn.shape[longest]
        spots.append(tuple(where))
    return drawn.at[spots[0]].set(low).at[spots[1]].set(top_value)


def setup_inputs(seed: int = 0) -> dict:
    seeds = jax.random.split(jax.random.key(seed), 7)
    return {
        "vectors": draw_vectors(jax.random.fold_in(seeds[6], 71), 0),
        "offsets": draw_offsets(jax.random.fold_in(seeds[6], 71), 0),
        "counts": with_ends(jax.random.randint(seeds[2], (ATOMS,), SLOTS // 2, SLOTS + 1), jax.random.fold_in(seeds[2], 1), SLOTS // 2, SLOTS).astype(jnp.int32),
        "labels": with_ends(jax.random.randint(seeds[3], (2, ATOMS), 0, 2), jax.random.fold_in(seeds[3], 1), 0, 1).astype(jnp.int32),
        "cosines": draw_cosines(jax.random.fold_in(seeds[6], 71), 0),
        "distances": draw_distances(jax.random.fold_in(seeds[6], 71), 0),
    }


PI_BOND = -1.0
SIGMA_BOND = 0.178
DECAY_LENGTH = 0.319
LAYER_GAP = 2.36
SITE_MASS = 0.4
LAYER_BIAS = 0.25

def hop_table(cosines, distances, counts):
    square = cosines * cosines
    bond_value = PI_BOND * jnp.exp(-(distances - 1.0) / DECAY_LENGTH) * (1.0 - square)
    bond_value = bond_value + SIGMA_BOND * jnp.exp(-(distances - LAYER_GAP) / DECAY_LENGTH) * square
    slot_index = lax.broadcasted_iota(jnp.int32, cosines.shape, 0)
    return jnp.where(slot_index < counts[None, :], bond_value, jnp.zeros_like(bond_value))

def onsite_of(labels):
    sublattice = (2 * labels[0] - 1).astype(jnp.float32)
    layer_sign = (2 * labels[1] - 1).astype(jnp.float32)
    return SITE_MASS * sublattice + LAYER_BIAS * layer_sign

def hamiltonian(source, hopping, offsets, onsite):
    atom_total = source.shape[1]
    column = jnp.arange(atom_total, dtype=jnp.int32)

    def advance(slot_index, running):
        target = (column + offsets[slot_index]) % atom_total
        return running + hopping[slot_index][None, :] * jnp.take(source, target, axis=1)
    return lax.fori_loop(0, hopping.shape[0], advance, onsite[None, :] * source)

def reference(vectors, offsets, counts, labels, cosines, distances):
    hopping = hop_table(cosines, distances, counts)
    onsite = onsite_of(labels)
    applied = hamiltonian(hamiltonian(vectors, hopping, offsets, onsite), hopping, offsets, onsite)
    blocks = [applied[block_index * BLOCK:(block_index + 1) * BLOCK] for block_index in range(NV // BLOCK)]
    highest = lax.Precision.HIGHEST
    for step_index in range(STEPS):
        gram_matrix = jnp.dot(blocks[step_index], blocks[step_index].T, precision=highest) / ATOMS
        factor = jnp.linalg.cholesky(gram_matrix)
        blocks[step_index] = jax.scipy.linalg.solve_triangular(factor, blocks[step_index], lower=True)
        for following in range(step_index + 1, len(blocks)):
            coupling = jnp.dot(blocks[step_index], blocks[following].T, precision=highest) / ATOMS
            blocks[following] = blocks[following] - jnp.dot(coupling.T, blocks[step_index], precision=highest)
    return jnp.concatenate(blocks, axis=0)
```

```python
import functools

import jax
import jax.numpy as jnp
from jax import lax
from jax.experimental import pallas as pl
from jax.experimental.pallas import tpu as pltpu
from jax.sharding import PartitionSpec as P

REACH = 256


PI_BOND = -1.0
SIGMA_BOND = 0.178
DECAY_LENGTH = 0.319
LAYER_GAP = 2.36
SITE_MASS = 0.4
LAYER_BIAS = 0.25


def extended_2(block, sides, width):
    for axis, dim in sides:
        count = lax.axis_size(axis)
        forward = [(i, i + 1) for i in range(count - 1)]
        forward.append((count - 1, 0))
        backward = [(target, source) for source, target in forward]
        low = lax.ppermute(
            lax.slice_in_dim(block, block.shape[dim] - width, None, axis=dim), axis, forward
        )
        high = lax.ppermute(lax.slice_in_dim(block, 0, width, axis=dim), axis, backward)
        block = jnp.concatenate([low, block, high], axis=dim)
    return block


def spread(value, axis, source):
    kept = jnp.where(lax.axis_index(axis) == source, value, 0).astype(value.dtype)
    return lax.psum(kept, axis)


def hop_table(cosines, distances, counts):
    square = cosines * cosines
    bond_value = PI_BOND * jnp.exp(-(distances - 1.0) / DECAY_LENGTH) * (1.0 - square)
    bond_value = bond_value + SIGMA_BOND * jnp.exp(-(distances - LAYER_GAP) / DECAY_LENGTH) * square
    slot_index = lax.broadcasted_iota(jnp.int32, cosines.shape, 0)
    return jnp.where(slot_index < counts[None, :], bond_value, jnp.zeros_like(bond_value))


def onsite_of(labels):
    sublattice = (2 * labels[0] - 1).astype(jnp.float32)
    layer_sign = (2 * labels[1] - 1).astype(jnp.float32)
    return SITE_MASS * sublattice + LAYER_BIAS * layer_sign


def apply_local(extended, hopping, offsets, onsite):
    atom_count = hopping.shape[1]
    middle = extended[:, REACH : REACH + atom_count]
    column = jnp.arange(atom_count, dtype=jnp.int32) + REACH

    def advance(slot_index, running):
        target = column + offsets[slot_index]
        return running + hopping[slot_index][None, :] * jnp.take(extended, target, axis=1)

    return lax.fori_loop(0, hopping.shape[0], advance, onsite[None, :] * middle)


def regroup(source):
    return lax.all_to_all(source, "cols", split_axis=0, concat_axis=1, tiled=True)


def on_device(vectors, offsets, counts, labels, cosines, distances):
    highest = lax.Precision.HIGHEST
    hopping = hop_table(cosines, distances, counts)
    onsite = onsite_of(labels)
    applied = vectors
    for repeat in range(2):
        extended = extended_2(applied, ((("rows", "cols"), 1),), REACH)
        applied = apply_local(extended, hopping, offsets, onsite)
    local_block = regroup(applied)
    atom_total = local_block.shape[1] * lax.axis_size("rows")
    step_count = min(3, lax.axis_size("cols") - 1)
    column_index = lax.axis_index("cols")
    for step_index in range(step_count):
        gram_matrix = (
            lax.psum(jnp.dot(local_block, local_block.T, precision=highest), "rows") / atom_total
        )
        factor = jnp.linalg.cholesky(gram_matrix)
        candidate = jax.scipy.linalg.solve_triangular(factor, local_block, lower=True)
        leader = spread(candidate, "cols", step_index)
        coupling = lax.psum(jnp.dot(leader, local_block.T, precision=highest), "rows") / atom_total
        reduced = local_block - jnp.dot(coupling.T, leader, precision=highest)
        local_block = jnp.where(
            column_index > step_index,
            reduced,
            jnp.where(column_index == step_index, leader, local_block),
        )
    return local_block


BLOCK = 64
TILE = 256
SPAN = TILE + 2 * REACH
HALF = 128
BAND = HALF + 2 * REACH
MESH = pl.DeviceIdType.MESH


def split_2(value):
    high = value.astype(jnp.bfloat16)
    low = (value - high.astype(jnp.float32)).astype(jnp.bfloat16)
    return high, low


def dot_nn(left, right):
    return lax.dot_general(
        left, right, (((1,), (0,)), ((), ())), preferred_element_type=jnp.float32
    )


def dot_nt(left, right):
    return lax.dot_general(
        left, right, (((1,), (1,)), ((), ())), preferred_element_type=jnp.float32
    )


def inverse_factor(gram):
    size = gram.shape[0]
    rows = lax.broadcasted_iota(jnp.int32, (size, size), 0)
    lanes = lax.broadcasted_iota(jnp.int32, (size, size), 1)
    eye = jnp.where(rows == lanes, 1.0, 0.0).astype(jnp.float32)
    wide = jnp.concatenate([gram, eye], axis=1)
    parts = [wide[8 * b : 8 * b + 8, :] for b in range(size // 8)]
    sub = lax.broadcasted_iota(jnp.int32, (8, 1), 0)
    for k in range(size - 1):
        b, s = k // 8, k % 8
        row = parts[b][s : s + 1, :]
        scaled = row * (1.0 / row[:, k : k + 1])
        for i in range(b, size // 8):
            column = parts[i][:, k : k + 1]
            if i == b:
                column = jnp.where(sub > s, column, 0.0)
            parts[i] = parts[i] - column * scaled
    done = jnp.concatenate(parts, axis=0)
    pivots = jnp.sum(jnp.where(rows == lanes, done[:, :size], 0.0), axis=1, keepdims=True)
    return done[:, size:] / jnp.sqrt(pivots)


def kernel(
    row_count, col_count, atom_total,
    v_ref, off_ref, cnt_ref, lab_ref, cos_ref, dist_ref, out_ref,
    key, hop, site, w_high, w_low, ext, mid, fin, halo, gram, rs, slab, zs, tot, gat, swap,
    send, recv,
):
    vector_count, local = v_ref.shape
    tiles = local // TILE
    planes = row_count // 4
    r, c = lax.axis_index("rows"), lax.axis_index("cols")
    place = r * col_count + c
    total = row_count * col_count
    ahead = lax.rem(place + 1, total)
    behind = lax.rem(place + total - 1, total)
    right = (ahead // col_count, lax.rem(ahead, col_count))
    left = (behind // col_count, lax.rem(behind, col_count))
    bit0, bit1 = lax.rem(r, 2), lax.rem(r // 2, 2)
    z = r // 4
    mine = c + 2 * lax.rem(r, 4)

    group = []
    for j in range(1, 8):
        pc = 1 - c if j & 1 else c
        p0 = 1 - bit0 if j & 2 else bit0
        p1 = 1 - bit1 if j & 4 else bit1
        group.append(((4 * z + 2 * p1 + p0, pc), pc + 2 * p0 + 4 * p1))
    peers = [
        (4 * lax.rem(z + d, planes) + lax.rem(r, 4), c) for d in range(1, planes)
    ]

    barrier = pltpu.get_barrier_semaphore()
    greeted = [left, right] + [g[0] for g in group] + peers
    for device in greeted:
        pl.semaphore_signal(barrier, inc=1, device_id=device, device_id_type=MESH)
    pl.semaphore_wait(barrier, len(greeted))

    def remote(slot, source, target, device):
        return pltpu.make_async_remote_copy(
            src_ref=source, dst_ref=target, send_sem=send.at[slot], recv_sem=recv.at[slot],
            device_id=device, device_id_type=MESH,
        )

    def edges(source, first):
        low = source.at[:, pl.ds(local - REACH, REACH)]
        high = source.at[:, pl.ds(0, REACH)]
        to_right = remote(first, low, halo.at[first], right)
        to_left = remote(first + 1, high, halo.at[first + 1], left)
        to_right.start()
        to_left.start()
        return to_right, to_left

    halo_a = edges(v_ref, 0)

    lane = lax.broadcasted_iota(jnp.int32, (1, local), 1)
    key[...] = off_ref[...] + (lax.rem(lane, HALF) + REACH)
    hop[...] = hop_table_2(cos_ref[...], dist_ref[...], cnt_ref[...])
    lab = lab_ref[...]
    signs = (2 * lab - 1).astype(jnp.float32)
    site[...] = SITE_MASS * signs[0:1, :] + LAYER_BIAS * signs[1:2, :]

    def put_ext(value, first, width):
        high, low = split_2(value)
        ext[0:vector_count, first : first + width] = high
        ext[vector_count : 2 * vector_count, first : first + width] = low

    put_ext(v_ref[...], REACH, local)

    slots = off_ref.shape[0]
    chunk = 32
    row8 = lax.broadcasted_iota(jnp.int32, (8, HALF), 0)

    def build(t, carry):
        for half in range(2):
            lanes = pl.ds(pl.multiple_of(t * TILE + half * HALF, HALF), HALF)
            keys = key[:, lanes]
            hops = hop[:, lanes]
            keys = [jnp.broadcast_to(keys[k : k + 1, :], (8, HALF)) for k in range(slots)]
            hops = [jnp.broadcast_to(hops[k : k + 1, :], (8, HALF)) for k in range(slots)]

            def rows(q, inner):
                parts = []
                for piece in range(chunk // 8):
                    index = row8 + (q * chunk + piece * 8)
                    terms = jnp.where(keys[0] == index, hops[0], 0.0)
                    for k in range(1, slots):
                        terms = terms + jnp.where(keys[k] == index, hops[k], 0.0)
                    parts.append(terms)
                high, low = split_2(jnp.concatenate(parts, axis=0))
                where = pl.ds(pl.multiple_of(q * chunk + half * HALF, chunk), chunk)
                span = pl.ds(half * HALF, HALF)
                w_high[t, where, span] = high
                w_low[t, where, span] = low
                return inner

            lax.fori_loop(0, BAND // chunk, rows, 0)
            blank = jnp.zeros((HALF, HALF), jnp.bfloat16)
            edge = pl.ds(BAND if half == 0 else 0, HALF)
            w_high[t, edge, pl.ds(half * HALF, HALF)] = blank
            w_low[t, edge, pl.ds(half * HALF, HALF)] = blank
        return carry

    lax.fori_loop(0, tiles, build, 0)

    def apply(t, source, target):
        lanes = slice(t * TILE, (t + 1) * TILE)
        span = slice(t * TILE, t * TILE + SPAN)
        both = dot_nn(ext[:, span], w_high[t])
        value = both[0:vector_count] + both[vector_count:]
        value = value + dot_nn(ext[0:vector_count, span], w_low[t])
        target[:, lanes] = value + site[:, lanes] * source[:, lanes]

    def finish(source, target, arrivals, first):
        to_right, to_left = arrivals
        for t in range(1, tiles - 1):
            apply(t, source, target)
        to_right.wait_recv()
        put_ext(halo[first], 0, REACH)
        apply(0, source, target)
        to_left.wait_recv()
        put_ext(halo[first + 1], REACH + local, REACH)
        apply(tiles - 1, source, target)

    finish(v_ref, mid, halo_a, 0)
    halo_b = edges(mid, 2)
    put_ext(mid[...], REACH, local)
    finish(mid, fin, halo_b, 2)

    high, low = split_2(fin[...])
    lead = jnp.concatenate([high[0:BLOCK], low[0:BLOCK]], axis=0)
    pair = dot_nt(lead, jnp.concatenate([high, low], axis=0))
    part = pair[0:BLOCK, 0:vector_count] + (
        pair[BLOCK:, 0:vector_count] + pair[0:BLOCK, vector_count:]
    )
    part = part * (1.0 / atom_total)
    for b in range(8):
        gram[b] = part[8 * b : 8 * b + 8, :]

    first = 4
    scatter = []
    for j in range(7):
        device, index = group[j]
        copy = remote(first + j, gram.at[index], rs.at[j], device)
        copy.start()
        scatter.append(copy)

    partner = (r, 1 - c)
    swap_a = remote(28, fin.at[pl.ds(0, BLOCK)], swap.at[pl.ds(0, BLOCK)], partner)
    swap_b = remote(29, fin.at[pl.ds(BLOCK, BLOCK)], swap.at[pl.ds(BLOCK, BLOCK)], partner)
    swap_a.start()

    @pl.when(c == 0)
    def _():
        swap_b.start()

    value = gram[mine]
    for j in range(7):
        scatter[j].wait_recv()
        value = value + rs[j]
    slab[...] = value
    across = []
    for d in range(planes - 1):
        copy = remote(11 + d, slab, zs.at[d], peers[d])
        copy.start()
        across.append(copy)
    for d in range(planes - 1):
        across[d].wait_recv()
        value = value + zs[d]
    tot[...] = value
    gather = []
    for j in range(7):
        copy = remote(21 + j, tot, gat.at[mine], group[j][0])
        copy.start()
        gather.append(copy)
    gat[mine] = value
    for j in range(7):
        gather[j].wait_recv()

    highest = lax.Precision.HIGHEST
    full = jnp.concatenate([gat[b] for b in range(8)], axis=0)
    inverse = inverse_factor(full[:, 0:BLOCK])
    coupling = jnp.dot(
        inverse, full[:, BLOCK:], precision=highest, preferred_element_type=jnp.float32
    )
    update = lax.dot_general(
        coupling, inverse, (((0,), (0,)), ((), ())), precision=highest,
        preferred_element_type=jnp.float32,
    )
    owner = c == 0
    factor_high, factor_low = split_2(jnp.where(owner, inverse, -update))
    factor = jnp.concatenate([factor_high, factor_low], axis=0)

    def result(lead_high, lead_low, own):
        both = dot_nn(factor, lead_high)
        value = both[0:BLOCK] + both[BLOCK:] + dot_nn(factor_high, lead_low)
        return value + jnp.where(owner, 0.0, own)

    own = result(high[0:BLOCK], low[0:BLOCK], fin[BLOCK:, :])
    out_ref[:, pl.ds(pl.multiple_of(c * local, local), local)] = own

    swap_a.wait_recv()

    @pl.when(c == 1)
    def _():
        swap_b.wait_recv()

    other_high, other_low = split_2(swap[0:BLOCK, :])
    theirs = result(other_high, other_low, swap[BLOCK:, :])
    out_ref[:, pl.ds(pl.multiple_of((1 - c) * local, local), local)] = theirs

    for copy in (*halo_a, *halo_b, *scatter, *across, *gather, swap_a):
        copy.wait_send()

    @pl.when(c == 0)
    def _():
        swap_b.wait_send()


def hop_table_2(cosines, distances, counts):
    square = cosines * cosines
    bond_value = PI_BOND * jnp.exp(-(distances - 1.0) / DECAY_LENGTH) * (1.0 - square)
    bond_value = bond_value + SIGMA_BOND * jnp.exp(-(distances - LAYER_GAP) / DECAY_LENGTH) * square
    slot_index = lax.broadcasted_iota(jnp.int32, cosines.shape, 0)
    return jnp.where(slot_index < counts, bond_value, jnp.zeros_like(bond_value))


def fused(row_count, col_count, vectors, offsets, counts, labels, cosines, distances):
    vector_count, local = vectors.shape
    slots = offsets.shape[0]
    tiles = local // TILE
    planes = row_count // 4
    f32, bf16 = jnp.float32, jnp.bfloat16
    vmem = pl.BlockSpec(memory_space=pltpu.VMEM)
    return pl.pallas_call(
        functools.partial(kernel, row_count, col_count, local * row_count * col_count),
        out_shape=jax.ShapeDtypeStruct((BLOCK, local * col_count), f32),
        in_specs=[vmem] * 6,
        out_specs=vmem,
        scratch_shapes=[
            pltpu.VMEM((slots, local), jnp.int32),
            pltpu.VMEM((slots, local), f32),
            pltpu.VMEM((1, local), f32),
            pltpu.VMEM((tiles, SPAN, TILE), bf16),
            pltpu.VMEM((tiles, SPAN, TILE), bf16),
            pltpu.VMEM((2 * vector_count, local + 2 * REACH), bf16),
            pltpu.VMEM((vector_count, local), f32),
            pltpu.VMEM((vector_count, local), f32),
            pltpu.VMEM((4, vector_count, REACH), f32),
            pltpu.VMEM((8, 8, vector_count), f32),
            pltpu.VMEM((7, 8, vector_count), f32),
            pltpu.VMEM((8, vector_count), f32),
            pltpu.VMEM((planes - 1, 8, vector_count), f32),
            pltpu.VMEM((8, vector_count), f32),
            pltpu.VMEM((8, 8, vector_count), f32),
            pltpu.VMEM((vector_count, local), f32),
            pltpu.SemaphoreType.DMA((30,)),
            pltpu.SemaphoreType.DMA((30,)),
        ],
        compiler_params=pltpu.CompilerParams(
            collective_id=0, has_side_effects=True, vmem_limit_bytes=40 * 1024 * 1024
        ),
    )(vectors, offsets, counts.reshape(1, local), labels, cosines, distances)


def fits(row_count, col_count, vectors):
    vector_count, local = vectors.shape
    return (
        col_count == 2
        and row_count in (8, 12, 16, 20, 24, 28, 32)
        and vector_count == 2 * BLOCK
        and local % TILE == 0
        and local >= 2 * TILE
    )


def on_slice(row_count, col_count, *arguments):
    if fits(row_count, col_count, arguments[0]):
        return fused(row_count, col_count, *arguments)
    return on_device(*arguments)


def solution(mesh):
    placed = (
        P(None, ("rows", "cols")),
        P(None, ("rows", "cols")),
        P(("rows", "cols")),
        P(None, ("rows", "cols")),
        P(None, ("rows", "cols")),
        P(None, ("rows", "cols")),
    )
    return jax.shard_map(
        functools.partial(on_slice, mesh.shape["rows"], mesh.shape["cols"]),
        mesh=mesh, in_specs=placed, out_specs=P("cols", "rows"), check_vma=False
    )
```

```python
import functools

import jax
import jax.numpy as jnp
from jax import lax
from jax.experimental import pallas as pl
from jax.experimental.pallas import tpu as pltpu
from jax.sharding import PartitionSpec as P

REACH = 256


PI_BOND = -1.0
SIGMA_BOND = 0.178
DECAY_LENGTH = 0.319
LAYER_GAP = 2.36
SITE_MASS = 0.4
LAYER_BIAS = 0.25


def extended_2(block, sides, width):
    for axis, dim in sides:
        count = lax.axis_size(axis)
        forward = [(i, i + 1) for i in range(count - 1)]
        forward.append((count - 1, 0))
        backward = [(target, source) for source, target in forward]
        low = lax.ppermute(
            lax.slice_in_dim(block, block.shape[dim] - width, None, axis=dim), axis, forward
        )
        high = lax.ppermute(lax.slice_in_dim(block, 0, width, axis=dim), axis, backward)
        block = jnp.concatenate([low, block, high], axis=dim)
    return block


def spread(value, axis, source):
    kept = jnp.where(lax.axis_index(axis) == source, value, 0).astype(value.dtype)
    return lax.psum(kept, axis)


def hop_table(cosines, distances, counts):
    square = cosines * cosines
    bond_value = PI_BOND * jnp.exp(-(distances - 1.0) / DECAY_LENGTH) * (1.0 - square)
    bond_value = bond_value + SIGMA_BOND * jnp.exp(-(distances - LAYER_GAP) / DECAY_LENGTH) * square
    slot_index = lax.broadcasted_iota(jnp.int32, cosines.shape, 0)
    return jnp.where(slot_index < counts[None, :], bond_value, jnp.zeros_like(bond_value))


def onsite_of(labels):
    sublattice = (2 * labels[0] - 1).astype(jnp.float32)
    layer_sign = (2 * labels[1] - 1).astype(jnp.float32)
    return SITE_MASS * sublattice + LAYER_BIAS * layer_sign


def apply_local(extended, hopping, offsets, onsite):
    atom_count = hopping.shape[1]
    middle = extended[:, REACH : REACH + atom_count]
    column = jnp.arange(atom_count, dtype=jnp.int32) + REACH

    def advance(slot_index, running):
        target = column + offsets[slot_index]
        return running + hopping[slot_index][None, :] * jnp.take(extended, target, axis=1)

    return lax.fori_loop(0, hopping.shape[0], advance, onsite[None, :] * middle)


def regroup(source):
    return lax.all_to_all(source, "cols", split_axis=0, concat_axis=1, tiled=True)


def on_device(vectors, offsets, counts, labels, cosines, distances):
    highest = lax.Precision.HIGHEST
    hopping = hop_table(cosines, distances, counts)
    onsite = onsite_of(labels)
    applied = vectors
    for repeat in range(2):
        extended = extended_2(applied, ((("rows", "cols"), 1),), REACH)
        applied = apply_local(extended, hopping, offsets, onsite)
    local_block = regroup(applied)
    atom_total = local_block.shape[1] * lax.axis_size("rows")
    step_count = min(3, lax.axis_size("cols") - 1)
    column_index = lax.axis_index("cols")
    for step_index in range(step_count):
        gram_matrix = (
            lax.psum(jnp.dot(local_block, local_block.T, precision=highest), "rows") / atom_total
        )
        factor = jnp.linalg.cholesky(gram_matrix)
        candidate = jax.scipy.linalg.solve_triangular(factor, local_block, lower=True)
        leader = spread(candidate, "cols", step_index)
        coupling = lax.psum(jnp.dot(leader, local_block.T, precision=highest), "rows") / atom_total
        reduced = local_block - jnp.dot(coupling.T, leader, precision=highest)
        local_block = jnp.where(
            column_index > step_index,
            reduced,
            jnp.where(column_index == step_index, leader, local_block),
        )
    return local_block


BLOCK = 64
TILE = 256
SPAN = TILE + 2 * REACH
HALF = 128
BAND = HALF + 2 * REACH
MESH = pl.DeviceIdType.MESH


def split_2(value):
    high = value.astype(jnp.bfloat16)
    low = (value - high.astype(jnp.float32)).astype(jnp.bfloat16)
    return high, low


def dot_nn(left, right):
    return lax.dot_general(
        left, right, (((1,), (0,)), ((), ())), preferred_element_type=jnp.float32
    )


def dot_nt(left, right):
    return lax.dot_general(
        left, right, (((1,), (1,)), ((), ())), preferred_element_type=jnp.float32
    )


def inverse_factor(gram):
    size = gram.shape[0]
    rows = lax.broadcasted_iota(jnp.int32, (size, size), 0)
    lanes = lax.broadcasted_iota(jnp.int32, (size, size), 1)
    eye = jnp.where(rows == lanes, 1.0, 0.0).astype(jnp.float32)
    wide = jnp.concatenate([gram, eye], axis=1)
    width = 2 * size
    count = size // 8
    parts = [wide[8 * b : 8 * b + 8, :] for b in range(count)]
    sub = lax.broadcasted_iota(jnp.int32, (8, width), 0)

    def lift(value, s):
        return jnp.broadcast_to(value[s : s + 1, :], (8, width))

    scales = []
    for b in range(count):
        columns = {
            i: [
                jnp.broadcast_to(parts[i][:, 8 * b + j : 8 * b + j + 1], (8, width))
                for j in range(8)
            ]
            for i in range(b, count)
        }
        lead = columns[b]
        for s in range(8):
            pivot = lift(lead[s], s)
            inverse = 1.0 / pivot
            if s == 0:
                scale = inverse
            else:
                scale = jnp.where(sub == s, inverse, scale)
            factors = {i: columns[i][s] * inverse for i in range(b, count)}
            factors[b] = jnp.where(sub > s, factors[b], 0.0)
            for j in range(s + 1, 8):
                top = lift(lead[j], s)
                for i in range(b, count):
                    columns[i][j] = columns[i][j] - factors[i] * top
            top = lift(parts[b], s)
            for i in range(b, count):
                parts[i] = parts[i] - factors[i] * top
        scales.append(scale)
    return jnp.concatenate(
        [(parts[b] * jnp.sqrt(scales[b]))[:, size:] for b in range(count)], axis=0
    )


def kernel(
    row_count, col_count, atom_total,
    v_hbm, off_hbm, cnt_hbm, lab_hbm, cos_hbm, dist_hbm, out_ref,
    v_ref, off_ref, cnt_ref, lab_ref, cos_ref, dist_ref,
    key, hop, site, w_high, w_low, ext, ext_2, mid, fin, halo, gram, rs, slab, zs, tot, gat, swap,
    send, recv, load,
):
    vector_count, local = v_ref.shape
    tiles = local // TILE
    planes = row_count // 4
    r, c = lax.axis_index("rows"), lax.axis_index("cols")
    place = r * col_count + c
    total = row_count * col_count
    ahead = lax.rem(place + 1, total)
    behind = lax.rem(place + total - 1, total)
    right = (ahead // col_count, lax.rem(ahead, col_count))
    left = (behind // col_count, lax.rem(behind, col_count))
    bit0, bit1 = lax.rem(r, 2), lax.rem(r // 2, 2)
    z = r // 4
    mine = lax.rem(r, 4)

    loads = [
        pltpu.make_async_copy(source, target, load.at[n])
        for n, (source, target) in enumerate((
            (off_hbm, off_ref), (cos_hbm, cos_ref), (dist_hbm, dist_ref),
            (cnt_hbm, cnt_ref), (lab_hbm, lab_ref), (v_hbm, v_ref),
        ))
    ]
    for copy in loads:
        copy.start()

    group = []
    for j in range(1, 4):
        p0 = 1 - bit0 if j & 1 else bit0
        p1 = 1 - bit1 if j & 2 else bit1
        group.append(((4 * z + 2 * p1 + p0, c), p0 + 2 * p1))
    peers = [
        (4 * lax.rem(z + d, planes) + lax.rem(r, 4), 1 - c if dx else c)
        for dx in range(2)
        for d in range(planes)
        if dx or d
    ]

    barrier = pltpu.get_barrier_semaphore()
    greeted = [left, right] + [g[0] for g in group] + peers
    for device in greeted:
        pl.semaphore_signal(barrier, inc=1, device_id=device, device_id_type=MESH)
    pl.semaphore_wait(barrier, len(greeted))

    def remote(slot, source, target, device):
        return pltpu.make_async_remote_copy(
            src_ref=source, dst_ref=target, send_sem=send.at[slot], recv_sem=recv.at[slot],
            device_id=device, device_id_type=MESH,
        )

    def edges(source, first):
        low = source.at[:, pl.ds(local - REACH, REACH)]
        high = source.at[:, pl.ds(0, REACH)]
        to_right = remote(first, low, halo.at[first], right)
        to_left = remote(first + 1, high, halo.at[first + 1], left)
        to_right.start()
        to_left.start()
        return to_right, to_left

    halo_a = edges(v_hbm, 0)

    for copy in loads[:5]:
        copy.wait()
    lane = lax.broadcasted_iota(jnp.int32, (1, local), 1)
    key[...] = off_ref[...] + (lax.rem(lane, HALF) + REACH)
    hop[...] = hop_table_2(cos_ref[...], dist_ref[...], cnt_ref[...])
    lab = lab_ref[...]
    signs = (2 * lab - 1).astype(jnp.float32)
    site[...] = SITE_MASS * signs[0:1, :] + LAYER_BIAS * signs[1:2, :]

    def put_ext(target, value, first, width):
        high, low = split_2(value)
        target[0:vector_count, first : first + width] = high
        target[vector_count : 2 * vector_count, first : first + width] = low

    slots = off_ref.shape[0]
    chunk = 32
    row8 = lax.broadcasted_iota(jnp.int32, (8, HALF), 0)

    def build(t):
        for half in range(2):
            lanes = pl.ds(pl.multiple_of(t * TILE + half * HALF, HALF), HALF)
            keys = key[:, lanes]
            hops = hop[:, lanes]
            keys = [jnp.broadcast_to(keys[k : k + 1, :], (8, HALF)) for k in range(slots)]
            hops = [jnp.broadcast_to(hops[k : k + 1, :], (8, HALF)) for k in range(slots)]

            def rows(q, inner):
                parts = []
                for piece in range(chunk // 8):
                    index = row8 + (q * chunk + piece * 8)
                    terms = jnp.where(keys[0] == index, hops[0], 0.0)
                    for k in range(1, slots):
                        terms = terms + jnp.where(keys[k] == index, hops[k], 0.0)
                    parts.append(terms)
                high, low = split_2(jnp.concatenate(parts, axis=0))
                where = pl.ds(pl.multiple_of(q * chunk + half * HALF, chunk), chunk)
                span = pl.ds(half * HALF, HALF)
                w_high[t, where, span] = high
                w_low[t, where, span] = low
                return inner

            lax.fori_loop(0, BAND // chunk, rows, 0)
            blank = jnp.zeros((HALF, HALF), jnp.bfloat16)
            edge = pl.ds(BAND if half == 0 else 0, HALF)
            w_high[t, edge, pl.ds(half * HALF, HALF)] = blank
            w_low[t, edge, pl.ds(half * HALF, HALF)] = blank

    def build_edge(n, carry):
        build(n * (tiles - 1))
        return carry

    def build_inner(n, carry):
        build(n)
        return carry

    lax.fori_loop(0, 2, build_edge, 0)

    def apply(t, ext, source, target):
        lanes = slice(t * TILE, (t + 1) * TILE)
        span = slice(t * TILE, t * TILE + SPAN)
        both = dot_nn(ext[:, span], w_high[t])
        value = both[0:vector_count] + both[vector_count:]
        value = value + dot_nn(ext[0:vector_count, span], w_low[t])
        target[:, lanes] = value + site[:, lanes] * source[:, lanes]

    last = tiles - 1
    loads[5].wait()
    put_ext(ext, v_ref[...], REACH, local)
    halo_a[0].wait_recv()
    halo_a[1].wait_recv()
    put_ext(ext, halo[0], 0, REACH)
    put_ext(ext, halo[1], REACH + local, REACH)
    apply(0, ext, v_ref, mid)
    apply(last, ext, v_ref, mid)
    halo_b = edges(mid, 2)

    lax.fori_loop(1, last, build_inner, 0)
    for t in range(1, last):
        apply(t, ext, v_ref, mid)
    put_ext(ext_2, mid[...], REACH, local)

    partner = (r, 1 - c)
    base = 20
    swaps = []

    def send_tile(t):
        pair = []
        for b in range(2):
            piece = (pl.ds(b * BLOCK, BLOCK), pl.ds(t * TILE, TILE))
            pair.append(
                remote(base + 2 * t + b, fin.at[piece], swap.at[piece], partner)
            )
        pair[0].start()

        @pl.when(c == 0)
        def _():
            pair[1].start()

        swaps.append((t, pair))

    for t in range(1, last):
        apply(t, ext_2, mid, fin)
        send_tile(t)
    halo_b[0].wait_recv()
    halo_b[1].wait_recv()
    put_ext(ext_2, halo[2], 0, REACH)
    put_ext(ext_2, halo[3], REACH + local, REACH)
    apply(0, ext_2, mid, fin)
    apply(last, ext_2, mid, fin)

    high, low = split_2(fin[...])
    lead = jnp.concatenate([high[0:BLOCK], low[0:BLOCK]], axis=0)
    pair = dot_nt(lead, jnp.concatenate([high, low], axis=0))
    part = pair[0:BLOCK, 0:vector_count] + (
        pair[BLOCK:, 0:vector_count] + pair[0:BLOCK, vector_count:]
    )
    part = part * (1.0 / atom_total)
    for b in range(4):
        gram[b] = part[16 * b : 16 * b + 16, :]

    scatter = []
    for j in range(3):
        device, index = group[j]
        copy = remote(4 + j, gram.at[index], rs.at[j], device)
        copy.start()
        scatter.append(copy)
    send_tile(0)
    send_tile(last)

    value = gram[mine]
    for j in range(3):
        scatter[j].wait_recv()
        value = value + rs[j]
    slab[...] = value
    across = []
    first = base + 2 * tiles
    for d in range(len(peers)):
        copy = remote(first + d, slab, zs.at[d], peers[d])
        copy.start()
        across.append(copy)
    for d in range(len(peers)):
        across[d].wait_recv()
        value = value + zs[d]
    tot[...] = value
    gather = []
    for j in range(3):
        copy = remote(7 + j, tot, gat.at[mine], group[j][0])
        copy.start()
        gather.append(copy)
    gat[mine] = value
    for j in range(3):
        gather[j].wait_recv()

    highest = lax.Precision.HIGHEST
    full = jnp.concatenate([gat[b] for b in range(4)], axis=0)
    inverse = inverse_factor(full[:, 0:BLOCK])
    coupling = jnp.dot(
        inverse, full[:, BLOCK:], precision=highest, preferred_element_type=jnp.float32
    )
    update = lax.dot_general(
        coupling, inverse, (((0,), (0,)), ((), ())), precision=highest,
        preferred_element_type=jnp.float32,
    )
    owner = c == 0
    factor_high, factor_low = split_2(jnp.where(owner, inverse, -update))
    factor = jnp.concatenate([factor_high, factor_low], axis=0)

    def result(lead_high, lead_low, own):
        both = dot_nn(factor, lead_high)
        value = both[0:BLOCK] + both[BLOCK:] + dot_nn(factor_high, lead_low)
        return value + jnp.where(owner, 0.0, own)

    own = result(high[0:BLOCK], low[0:BLOCK], fin[BLOCK:, :])
    out_ref[:, pl.ds(pl.multiple_of(c * local, local), local)] = own

    there = pl.multiple_of((1 - c) * local, local)
    for t, pair in swaps:
        pair[0].wait_recv()

        @pl.when(c == 1)
        def _():
            pair[1].wait_recv()

        lanes = slice(t * TILE, (t + 1) * TILE)
        other_high, other_low = split_2(swap[0:BLOCK, lanes])
        theirs = result(other_high, other_low, swap[BLOCK:, lanes])
        out_ref[:, pl.ds(pl.multiple_of(there + t * TILE, TILE), TILE)] = theirs

    for copy in (*halo_a, *halo_b, *scatter, *across, *gather):
        copy.wait_send()
    for t, pair in swaps:
        pair[0].wait_send()

        @pl.when(c == 0)
        def _():
            pair[1].wait_send()


def hop_table_2(cosines, distances, counts):
    square = cosines * cosines
    bond_value = PI_BOND * jnp.exp(-(distances - 1.0) / DECAY_LENGTH) * (1.0 - square)
    bond_value = bond_value + SIGMA_BOND * jnp.exp(-(distances - LAYER_GAP) / DECAY_LENGTH) * square
    slot_index = lax.broadcasted_iota(jnp.int32, cosines.shape, 0)
    return jnp.where(slot_index < counts, bond_value, jnp.zeros_like(bond_value))


def fused(row_count, col_count, vectors, offsets, counts, labels, cosines, distances):
    vector_count, local = vectors.shape
    slots = offsets.shape[0]
    tiles = local // TILE
    planes = row_count // 4
    f32, bf16 = jnp.float32, jnp.bfloat16
    vmem = pl.BlockSpec(memory_space=pltpu.VMEM)
    peers = 2 * planes - 1
    semaphores = 20 + 2 * tiles + peers
    return pl.pallas_call(
        functools.partial(kernel, row_count, col_count, local * row_count * col_count),
        out_shape=jax.ShapeDtypeStruct((BLOCK, local * col_count), f32),
        in_specs=[pl.BlockSpec(memory_space=pltpu.HBM)] * 6,
        out_specs=vmem,
        scratch_shapes=[
            pltpu.VMEM((vector_count, local), f32),
            pltpu.VMEM((slots, local), jnp.int32),
            pltpu.VMEM((1, local), jnp.int32),
            pltpu.VMEM((2, local), jnp.int32),
            pltpu.VMEM((slots, local), f32),
            pltpu.VMEM((slots, local), f32),
            pltpu.VMEM((slots, local), jnp.int32),
            pltpu.VMEM((slots, local), f32),
            pltpu.VMEM((1, local), f32),
            pltpu.VMEM((tiles, SPAN, TILE), bf16),
            pltpu.VMEM((tiles, SPAN, TILE), bf16),
            pltpu.VMEM((2 * vector_count, local + 2 * REACH), bf16),
            pltpu.VMEM((2 * vector_count, local + 2 * REACH), bf16),
            pltpu.VMEM((vector_count, local), f32),
            pltpu.VMEM((vector_count, local), f32),
            pltpu.VMEM((4, vector_count, REACH), f32),
            pltpu.VMEM((4, 16, vector_count), f32),
            pltpu.VMEM((3, 16, vector_count), f32),
            pltpu.VMEM((16, vector_count), f32),
            pltpu.VMEM((peers, 16, vector_count), f32),
            pltpu.VMEM((16, vector_count), f32),
            pltpu.VMEM((4, 16, vector_count), f32),
            pltpu.VMEM((vector_count, local), f32),
            pltpu.SemaphoreType.DMA((semaphores,)),
            pltpu.SemaphoreType.DMA((semaphores,)),
            pltpu.SemaphoreType.DMA((6,)),
        ],
        compiler_params=pltpu.CompilerParams(
            collective_id=0, has_side_effects=True, vmem_limit_bytes=60 * 1024 * 1024
        ),
    )(vectors, offsets, counts.reshape(1, local), labels, cosines, distances)


def fits(row_count, col_count, vectors):
    vector_count, local = vectors.shape
    return (
        col_count == 2
        and row_count in (8, 12, 16, 20, 24, 28, 32)
        and vector_count == 2 * BLOCK
        and local % TILE == 0
        and local >= 2 * TILE
    )


def on_slice(row_count, col_count, *arguments):
    if fits(row_count, col_count, arguments[0]):
        return fused(row_count, col_count, *arguments)
    return on_device(*arguments)


def solution(mesh):
    placed = (
        P(None, ("rows", "cols")),
        P(None, ("rows", "cols")),
        P(("rows", "cols")),
        P(None, ("rows", "cols")),
        P(None, ("rows", "cols")),
        P(None, ("rows", "cols")),
    )
    return jax.shard_map(
        functools.partial(on_slice, mesh.shape["rows"], mesh.shape["cols"]),
        mesh=mesh, in_specs=placed, out_specs=P("cols", "rows"), check_vma=False
    )
```

```python
import functools

import jax
import jax.numpy as jnp
from jax import lax
from jax.experimental import pallas as pl
from jax.experimental.pallas import tpu as pltpu
from jax.sharding import PartitionSpec as P

REACH = 256


PI_BOND = -1.0
SIGMA_BOND = 0.178
DECAY_LENGTH = 0.319
LAYER_GAP = 2.36
SITE_MASS = 0.4
LAYER_BIAS = 0.25


def extended_2(block, sides, width):
    for axis, dim in sides:
        count = lax.axis_size(axis)
        forward = [(i, i + 1) for i in range(count - 1)]
        forward.append((count - 1, 0))
        backward = [(target, source) for source, target in forward]
        low = lax.ppermute(
            lax.slice_in_dim(block, block.shape[dim] - width, None, axis=dim), axis, forward
        )
        high = lax.ppermute(lax.slice_in_dim(block, 0, width, axis=dim), axis, backward)
        block = jnp.concatenate([low, block, high], axis=dim)
    return block


def spread(value, axis, source):
    kept = jnp.where(lax.axis_index(axis) == source, value, 0).astype(value.dtype)
    return lax.psum(kept, axis)


def hop_table(cosines, distances, counts):
    square = cosines * cosines
    bond_value = PI_BOND * jnp.exp(-(distances - 1.0) / DECAY_LENGTH) * (1.0 - square)
    bond_value = bond_value + SIGMA_BOND * jnp.exp(-(distances - LAYER_GAP) / DECAY_LENGTH) * square
    slot_index = lax.broadcasted_iota(jnp.int32, cosines.shape, 0)
    return jnp.where(slot_index < counts[None, :], bond_value, jnp.zeros_like(bond_value))


def onsite_of(labels):
    sublattice = (2 * labels[0] - 1).astype(jnp.float32)
    layer_sign = (2 * labels[1] - 1).astype(jnp.float32)
    return SITE_MASS * sublattice + LAYER_BIAS * layer_sign


def apply_local(extended, hopping, offsets, onsite):
    atom_count = hopping.shape[1]
    middle = extended[:, REACH : REACH + atom_count]
    column = jnp.arange(atom_count, dtype=jnp.int32) + REACH

    def advance(slot_index, running):
        target = column + offsets[slot_index]
        return running + hopping[slot_index][None, :] * jnp.take(extended, target, axis=1)

    return lax.fori_loop(0, hopping.shape[0], advance, onsite[None, :] * middle)


def regroup(source):
    return lax.all_to_all(source, "cols", split_axis=0, concat_axis=1, tiled=True)


def on_device(vectors, offsets, counts, labels, cosines, distances):
    highest = lax.Precision.HIGHEST
    hopping = hop_table(cosines, distances, counts)
    onsite = onsite_of(labels)
    applied = vectors
    for repeat in range(2):
        extended = extended_2(applied, ((("rows", "cols"), 1),), REACH)
        applied = apply_local(extended, hopping, offsets, onsite)
    local_block = regroup(applied)
    atom_total = local_block.shape[1] * lax.axis_size("rows")
    step_count = min(3, lax.axis_size("cols") - 1)
    column_index = lax.axis_index("cols")
    for step_index in range(step_count):
        gram_matrix = (
            lax.psum(jnp.dot(local_block, local_block.T, precision=highest), "rows") / atom_total
        )
        factor = jnp.linalg.cholesky(gram_matrix)
        candidate = jax.scipy.linalg.solve_triangular(factor, local_block, lower=True)
        leader = spread(candidate, "cols", step_index)
        coupling = lax.psum(jnp.dot(leader, local_block.T, precision=highest), "rows") / atom_total
        reduced = local_block - jnp.dot(coupling.T, leader, precision=highest)
        local_block = jnp.where(
            column_index > step_index,
            reduced,
            jnp.where(column_index == step_index, leader, local_block),
        )
    return local_block


BLOCK = 64
TILE = 256
SPAN = TILE + 2 * REACH
HALF = 128
BAND = HALF + 2 * REACH
MESH = pl.DeviceIdType.MESH


def split_2(value):
    high = value.astype(jnp.bfloat16)
    low = (value - high.astype(jnp.float32)).astype(jnp.bfloat16)
    return high, low


def dot_nn(left, right):
    return lax.dot_general(
        left, right, (((1,), (0,)), ((), ())), preferred_element_type=jnp.float32
    )


def dot_nt(left, right):
    return lax.dot_general(
        left, right, (((1,), (1,)), ((), ())), preferred_element_type=jnp.float32
    )


def inverse_factor(gram):
    size = gram.shape[0]
    rows = lax.broadcasted_iota(jnp.int32, (size, size), 0)
    lanes = lax.broadcasted_iota(jnp.int32, (size, size), 1)
    eye = jnp.where(rows == lanes, 1.0, 0.0).astype(jnp.float32)
    wide = jnp.concatenate([gram, eye], axis=1)
    width = 2 * size
    count = size // 8
    parts = [wide[8 * b : 8 * b + 8, :] for b in range(count)]
    sub = lax.broadcasted_iota(jnp.int32, (8, width), 0)

    def lift(value, s):
        return jnp.broadcast_to(value[s : s + 1, :], (8, width))

    scales = []
    for b in range(count):
        columns = {
            i: [
                jnp.broadcast_to(parts[i][:, 8 * b + j : 8 * b + j + 1], (8, width))
                for j in range(8)
            ]
            for i in range(b, count)
        }
        lead = columns[b]
        for s in range(8):
            pivot = lift(lead[s], s)
            inverse = 1.0 / pivot
            if s == 0:
                scale = inverse
            else:
                scale = jnp.where(sub == s, inverse, scale)
            factors = {i: columns[i][s] * inverse for i in range(b, count)}
            factors[b] = jnp.where(sub > s, factors[b], 0.0)
            for j in range(s + 1, 8):
                top = lift(lead[j], s)
                for i in range(b, count):
                    columns[i][j] = columns[i][j] - factors[i] * top
            top = lift(parts[b], s)
            for i in range(b, count):
                parts[i] = parts[i] - factors[i] * top
        scales.append(scale)
    return jnp.concatenate(
        [(parts[b] * jnp.sqrt(scales[b]))[:, size:] for b in range(count)], axis=0
    )


def kernel(
    row_count, col_count, atom_total,
    v_hbm, off_hbm, cnt_hbm, lab_hbm, cos_hbm, dist_hbm, out_ref,
    v_ref, off_ref, cnt_ref, lab_ref, cos_ref, dist_ref,
    key, hop, site, w_high, w_low, ext, ext_2, mid, fin, halo, gram, rs, slab, zs, tot, gat, swap,
    send, recv, load,
):
    vector_count, local = v_ref.shape
    tiles = local // TILE
    planes = row_count // 4
    r, c = lax.axis_index("rows"), lax.axis_index("cols")
    place = r * col_count + c
    total = row_count * col_count
    ahead = lax.rem(place + 1, total)
    behind = lax.rem(place + total - 1, total)
    right = (ahead // col_count, lax.rem(ahead, col_count))
    left = (behind // col_count, lax.rem(behind, col_count))
    bit0, bit1 = lax.rem(r, 2), lax.rem(r // 2, 2)
    z = r // 4
    mine = lax.rem(r, 4)

    loads = [
        pltpu.make_async_copy(source, target, load.at[n])
        for n, (source, target) in enumerate((
            (off_hbm, off_ref), (cos_hbm, cos_ref), (dist_hbm, dist_ref),
            (cnt_hbm, cnt_ref), (lab_hbm, lab_ref), (v_hbm, v_ref),
        ))
    ]
    for copy in loads:
        copy.start()

    group = []
    for j in range(1, 4):
        p0 = 1 - bit0 if j & 1 else bit0
        p1 = 1 - bit1 if j & 2 else bit1
        group.append(((4 * z + 2 * p1 + p0, c), p0 + 2 * p1))
    peers = [
        (4 * lax.rem(z + d, planes) + lax.rem(r, 4), 1 - c if dx else c)
        for dx in range(2)
        for d in range(planes)
        if dx or d
    ]

    barrier = pltpu.get_barrier_semaphore()
    greeted = [left, right] + [g[0] for g in group] + peers
    for device in greeted:
        pl.semaphore_signal(barrier, inc=1, device_id=device, device_id_type=MESH)

    def remote(slot, source, target, device):
        return pltpu.make_async_remote_copy(
            src_ref=source, dst_ref=target, send_sem=send.at[slot], recv_sem=recv.at[slot],
            device_id=device, device_id_type=MESH,
        )

    def edges(source, first):
        low = source.at[:, pl.ds(local - REACH, REACH)]
        high = source.at[:, pl.ds(0, REACH)]
        to_right = remote(first, low, halo.at[first], right)
        to_left = remote(first + 1, high, halo.at[first + 1], left)
        to_right.start()
        to_left.start()
        return to_right, to_left

    for copy in loads[:5]:
        copy.wait()
    lane = lax.broadcasted_iota(jnp.int32, (1, local), 1)
    keys_all, hops_all = merged(
        off_ref[...] + (lax.rem(lane, HALF) + REACH),
        hop_table_2(cos_ref[...], dist_ref[...], cnt_ref[...]),
    )
    key[...] = keys_all
    hop[...] = hops_all
    lab = lab_ref[...]
    signs = (2 * lab - 1).astype(jnp.float32)
    site[...] = SITE_MASS * signs[0:1, :] + LAYER_BIAS * signs[1:2, :]

    pl.semaphore_wait(barrier, len(greeted))
    halo_a = edges(v_hbm, 0)

    def put_ext(target, value, first, width):
        high, low = split_2(value)
        target[0:vector_count, first : first + width] = high
        target[vector_count : 2 * vector_count, first : first + width] = low

    slots = off_ref.shape[0]
    chunk = 64
    row16 = lax.broadcasted_iota(jnp.int32, (16, HALF), 0)

    def build(t):
        for half in range(2):
            lanes = pl.ds(pl.multiple_of(t * TILE + half * HALF, HALF), HALF)
            span = pl.ds(half * HALF, HALF)
            keys = key[:, lanes]
            hops = hop[:, lanes]
            keys = [
                jnp.broadcast_to(keys[k : k + 1, :], (16, HALF)).astype(jnp.int16)
                for k in range(slots)
            ]
            hops = [
                split_2(jnp.broadcast_to(hops[k : k + 1, :], (16, HALF))) for k in range(slots)
            ]

            def rows(q, inner):
                for piece in range(chunk // 16):
                    index = (row16 + (q * chunk + piece * 16)).astype(jnp.int16)
                    high = low = jnp.zeros((16, HALF), jnp.bfloat16)
                    for k in range(slots):
                        here = keys[k] == index
                        high = jnp.where(here, hops[k][0], high)
                        low = jnp.where(here, hops[k][1], low)
                    first = pl.multiple_of(q * chunk + piece * 16 + half * HALF, 16)
                    w_high[t, pl.ds(first, 16), span] = high
                    w_low[t, pl.ds(first, 16), span] = low
                return inner

            lax.fori_loop(0, BAND // chunk, rows, 0)
            blank = jnp.zeros((HALF, HALF), jnp.bfloat16)
            edge = pl.ds(BAND if half == 0 else 0, HALF)
            w_high[t, edge, pl.ds(half * HALF, HALF)] = blank
            w_low[t, edge, pl.ds(half * HALF, HALF)] = blank

    def build_edge(n, carry):
        build(n * (tiles - 1))
        return carry

    def build_inner(n, carry):
        build(n)
        return carry

    lax.fori_loop(0, 2, build_edge, 0)

    def apply(t, ext, source, target):
        lanes = slice(t * TILE, (t + 1) * TILE)
        span = slice(t * TILE, t * TILE + SPAN)
        both = dot_nn(ext[:, span], w_high[t])
        value = both[0:vector_count] + both[vector_count:]
        value = value + dot_nn(ext[0:vector_count, span], w_low[t])
        target[:, lanes] = value + site[:, lanes] * source[:, lanes]

    last = tiles - 1
    loads[5].wait()
    put_ext(ext, v_ref[...], REACH, local)
    halo_a[0].wait_recv()
    halo_a[1].wait_recv()
    put_ext(ext, halo[0], 0, REACH)
    put_ext(ext, halo[1], REACH + local, REACH)
    apply(0, ext, v_ref, mid)
    apply(last, ext, v_ref, mid)
    halo_b = edges(mid, 2)

    lax.fori_loop(1, last, build_inner, 0)
    for t in range(1, last):
        apply(t, ext, v_ref, mid)
    put_ext(ext_2, mid[...], REACH, local)

    partner = (r, 1 - c)
    base = 20
    swaps = []

    def send_tile(t):
        pair = []
        for b in range(2):
            piece = (pl.ds(b * BLOCK, BLOCK), pl.ds(t * TILE, TILE))
            pair.append(
                remote(base + 2 * t + b, fin.at[piece], swap.at[piece], partner)
            )
        pair[0].start()

        @pl.when(c == 0)
        def _():
            pair[1].start()

        swaps.append((t, pair))

    for t in range(1, last):
        apply(t, ext_2, mid, fin)
        send_tile(t)
    halo_b[0].wait_recv()
    halo_b[1].wait_recv()
    put_ext(ext_2, halo[2], 0, REACH)
    put_ext(ext_2, halo[3], REACH + local, REACH)
    apply(0, ext_2, mid, fin)
    apply(last, ext_2, mid, fin)

    high, low = split_2(fin[...])
    lead = jnp.concatenate([high[0:BLOCK], low[0:BLOCK]], axis=0)
    pair = dot_nt(lead, jnp.concatenate([high, low], axis=0))
    part = pair[0:BLOCK, 0:vector_count] + (
        pair[BLOCK:, 0:vector_count] + pair[0:BLOCK, vector_count:]
    )
    part = part * (1.0 / atom_total)
    for b in range(4):
        gram[b] = part[16 * b : 16 * b + 16, :]

    scatter = []
    for j in range(3):
        device, index = group[j]
        copy = remote(4 + j, gram.at[index], rs.at[j], device)
        copy.start()
        scatter.append(copy)
    send_tile(0)
    send_tile(last)

    value = gram[mine]
    for j in range(3):
        scatter[j].wait_recv()
        value = value + rs[j]
    slab[...] = value
    across = []
    first = base + 2 * tiles
    for d in range(len(peers)):
        copy = remote(first + d, slab, zs.at[d], peers[d])
        copy.start()
        across.append(copy)
    for d in range(len(peers)):
        across[d].wait_recv()
        value = value + zs[d]
    tot[...] = value
    gather = []
    for j in range(3):
        copy = remote(7 + j, tot, gat.at[mine], group[j][0])
        copy.start()
        gather.append(copy)
    gat[mine] = value
    for j in range(3):
        gather[j].wait_recv()

    highest = lax.Precision.HIGHEST
    full = jnp.concatenate([gat[b] for b in range(4)], axis=0)
    inverse = inverse_factor(full[:, 0:BLOCK])
    coupling = jnp.dot(
        inverse, full[:, BLOCK:], precision=highest, preferred_element_type=jnp.float32
    )
    update = lax.dot_general(
        coupling, inverse, (((0,), (0,)), ((), ())), precision=highest,
        preferred_element_type=jnp.float32,
    )
    owner = c == 0
    factor_high, factor_low = split_2(jnp.where(owner, inverse, -update))
    factor = jnp.concatenate([factor_high, factor_low], axis=0)

    def result(lead_high, lead_low, own):
        both = dot_nn(factor, lead_high)
        value = both[0:BLOCK] + both[BLOCK:] + dot_nn(factor_high, lead_low)
        return value + jnp.where(owner, 0.0, own)

    own = result(high[0:BLOCK], low[0:BLOCK], fin[BLOCK:, :])
    out_ref[:, pl.ds(pl.multiple_of(c * local, local), local)] = own

    there = pl.multiple_of((1 - c) * local, local)
    for t, pair in swaps:
        pair[0].wait_recv()

        @pl.when(c == 1)
        def _():
            pair[1].wait_recv()

        lanes = slice(t * TILE, (t + 1) * TILE)
        other_high, other_low = split_2(swap[0:BLOCK, lanes])
        theirs = result(other_high, other_low, swap[BLOCK:, lanes])
        out_ref[:, pl.ds(pl.multiple_of(there + t * TILE, TILE), TILE)] = theirs

    for copy in (*halo_a, *halo_b, *scatter, *across, *gather):
        copy.wait_send()
    for t, pair in swaps:
        pair[0].wait_send()

        @pl.when(c == 0)
        def _():
            pair[1].wait_send()


def merged(keys, values):
    count = keys.shape[0]
    row = lax.broadcasted_iota(jnp.int32, keys.shape, 0)
    repeated = jnp.zeros(keys.shape, jnp.int32)
    total = values
    for shift in range(1, count):
        near = jnp.concatenate([keys[count - shift :], keys[: count - shift]], axis=0)
        value = jnp.concatenate([values[count - shift :], values[: count - shift]], axis=0)
        same = near == keys
        later = row < shift
        total = total + jnp.where(same & later, value, 0.0)
        repeated = jnp.where(same & ~later, 1, repeated)
    return jnp.where(repeated == 1, -1, keys), total


def hop_table_2(cosines, distances, counts):
    square = cosines * cosines
    bond_value = PI_BOND * jnp.exp(-(distances - 1.0) / DECAY_LENGTH) * (1.0 - square)
    bond_value = bond_value + SIGMA_BOND * jnp.exp(-(distances - LAYER_GAP) / DECAY_LENGTH) * square
    slot_index = lax.broadcasted_iota(jnp.int32, cosines.shape, 0)
    return jnp.where(slot_index < counts, bond_value, jnp.zeros_like(bond_value))


def fused(row_count, col_count, vectors, offsets, counts, labels, cosines, distances):
    vector_count, local = vectors.shape
    slots = offsets.shape[0]
    tiles = local // TILE
    planes = row_count // 4
    f32, bf16 = jnp.float32, jnp.bfloat16
    vmem = pl.BlockSpec(memory_space=pltpu.VMEM)
    peers = 2 * planes - 1
    semaphores = 20 + 2 * tiles + peers
    return pl.pallas_call(
        functools.partial(kernel, row_count, col_count, local * row_count * col_count),
        out_shape=pltpu.VMEM((BLOCK, local * col_count), f32),
        in_specs=[pl.BlockSpec(memory_space=pltpu.HBM)] * 6,
        out_specs=vmem,
        scratch_shapes=[
            pltpu.VMEM((vector_count, local), f32),
            pltpu.VMEM((slots, local), jnp.int32),
            pltpu.VMEM((1, local), jnp.int32),
            pltpu.VMEM((2, local), jnp.int32),
            pltpu.VMEM((slots, local), f32),
            pltpu.VMEM((slots, local), f32),
            pltpu.VMEM((slots, local), jnp.int32),
            pltpu.VMEM((slots, local), f32),
            pltpu.VMEM((1, local), f32),
            pltpu.VMEM((tiles, SPAN, TILE), bf16),
            pltpu.VMEM((tiles, SPAN, TILE), bf16),
            pltpu.VMEM((2 * vector_count, local + 2 * REACH), bf16),
            pltpu.VMEM((2 * vector_count, local + 2 * REACH), bf16),
            pltpu.VMEM((vector_count, local), f32),
            pltpu.VMEM((vector_count, local), f32),
            pltpu.VMEM((4, vector_count, REACH), f32),
            pltpu.VMEM((4, 16, vector_count), f32),
            pltpu.VMEM((3, 16, vector_count), f32),
            pltpu.VMEM((16, vector_count), f32),
            pltpu.VMEM((peers, 16, vector_count), f32),
            pltpu.VMEM((16, vector_count), f32),
            pltpu.VMEM((4, 16, vector_count), f32),
            pltpu.VMEM((vector_count, local), f32),
            pltpu.SemaphoreType.DMA((semaphores,)),
            pltpu.SemaphoreType.DMA((semaphores,)),
            pltpu.SemaphoreType.DMA((6,)),
        ],
        compiler_params=pltpu.CompilerParams(
            collective_id=0, has_side_effects=True, vmem_limit_bytes=60 * 1024 * 1024
        ),
    )(vectors, offsets, counts.reshape(1, local), labels, cosines, distances)


def fits(row_count, col_count, vectors):
    vector_count, local = vectors.shape
    return (
        col_count == 2
        and row_count in (8, 12, 16, 20, 24, 28, 32)
        and vector_count == 2 * BLOCK
        and local % TILE == 0
        and local >= 2 * TILE
    )


def on_slice(row_count, col_count, *arguments):
    if fits(row_count, col_count, arguments[0]):
        return fused(row_count, col_count, *arguments)
    return on_device(*arguments)


def solution(mesh):
    placed = (
        P(None, ("rows", "cols")),
        P(None, ("rows", "cols")),
        P(("rows", "cols")),
        P(None, ("rows", "cols")),
        P(None, ("rows", "cols")),
        P(None, ("rows", "cols")),
    )
    return jax.shard_map(
        functools.partial(on_slice, mesh.shape["rows"], mesh.shape["cols"]),
        mesh=mesh, in_specs=placed, out_specs=P("cols", "rows"), check_vma=False
    )
```

```python
import functools

import jax
import jax.numpy as jnp
from jax import lax
from jax.experimental import pallas as pl
from jax.experimental.pallas import tpu as pltpu
from jax.sharding import PartitionSpec as P

REACH = 256


PI_BOND = -1.0
SIGMA_BOND = 0.178
DECAY_LENGTH = 0.319
LAYER_GAP = 2.36
SITE_MASS = 0.4
LAYER_BIAS = 0.25


def extended_2(block, sides, width):
    for axis, dim in sides:
        count = lax.axis_size(axis)
        forward = [(i, i + 1) for i in range(count - 1)]
        forward.append((count - 1, 0))
        backward = [(target, source) for source, target in forward]
        low = lax.ppermute(
            lax.slice_in_dim(block, block.shape[dim] - width, None, axis=dim), axis, forward
        )
        high = lax.ppermute(lax.slice_in_dim(block, 0, width, axis=dim), axis, backward)
        block = jnp.concatenate([low, block, high], axis=dim)
    return block


def spread(value, axis, source):
    kept = jnp.where(lax.axis_index(axis) == source, value, 0).astype(value.dtype)
    return lax.psum(kept, axis)


def hop_table(cosines, distances, counts):
    square = cosines * cosines
    bond_value = PI_BOND * jnp.exp(-(distances - 1.0) / DECAY_LENGTH) * (1.0 - square)
    bond_value = bond_value + SIGMA_BOND * jnp.exp(-(distances - LAYER_GAP) / DECAY_LENGTH) * square
    slot_index = lax.broadcasted_iota(jnp.int32, cosines.shape, 0)
    return jnp.where(slot_index < counts[None, :], bond_value, jnp.zeros_like(bond_value))


def onsite_of(labels):
    sublattice = (2 * labels[0] - 1).astype(jnp.float32)
    layer_sign = (2 * labels[1] - 1).astype(jnp.float32)
    return SITE_MASS * sublattice + LAYER_BIAS * layer_sign


def apply_local(extended, hopping, offsets, onsite):
    atom_count = hopping.shape[1]
    middle = extended[:, REACH : REACH + atom_count]
    column = jnp.arange(atom_count, dtype=jnp.int32) + REACH

    def advance(slot_index, running):
        target = column + offsets[slot_index]
        return running + hopping[slot_index][None, :] * jnp.take(extended, target, axis=1)

    return lax.fori_loop(0, hopping.shape[0], advance, onsite[None, :] * middle)


def regroup(source):
    return lax.all_to_all(source, "cols", split_axis=0, concat_axis=1, tiled=True)


def on_device(vectors, offsets, counts, labels, cosines, distances):
    highest = lax.Precision.HIGHEST
    hopping = hop_table(cosines, distances, counts)
    onsite = onsite_of(labels)
    applied = vectors
    for repeat in range(2):
        extended = extended_2(applied, ((("rows", "cols"), 1),), REACH)
        applied = apply_local(extended, hopping, offsets, onsite)
    local_block = regroup(applied)
    atom_total = local_block.shape[1] * lax.axis_size("rows")
    step_count = min(3, lax.axis_size("cols") - 1)
    column_index = lax.axis_index("cols")
    for step_index in range(step_count):
        gram_matrix = (
            lax.psum(jnp.dot(local_block, local_block.T, precision=highest), "rows") / atom_total
        )
        factor = jnp.linalg.cholesky(gram_matrix)
        candidate = jax.scipy.linalg.solve_triangular(factor, local_block, lower=True)
        leader = spread(candidate, "cols", step_index)
        coupling = lax.psum(jnp.dot(leader, local_block.T, precision=highest), "rows") / atom_total
        reduced = local_block - jnp.dot(coupling.T, leader, precision=highest)
        local_block = jnp.where(
            column_index > step_index,
            reduced,
            jnp.where(column_index == step_index, leader, local_block),
        )
    return local_block


BLOCK = 64
TILE = 256
SPAN = TILE + 2 * REACH
HALF = 128
BAND = HALF + 2 * REACH
MESH = pl.DeviceIdType.MESH


def split_2(value):
    high = value.astype(jnp.bfloat16)
    low = (value - high.astype(jnp.float32)).astype(jnp.bfloat16)
    return high, low


def dot_nn(left, right):
    return lax.dot_general(
        left, right, (((1,), (0,)), ((), ())), preferred_element_type=jnp.float32
    )


def dot_nt(left, right):
    return lax.dot_general(
        left, right, (((1,), (1,)), ((), ())), preferred_element_type=jnp.float32
    )


def inverse_factor(gram):
    size = gram.shape[0]
    rows = lax.broadcasted_iota(jnp.int32, (size, size), 0)
    lanes = lax.broadcasted_iota(jnp.int32, (size, size), 1)
    eye = jnp.where(rows == lanes, 1.0, 0.0).astype(jnp.float32)
    wide = jnp.concatenate([gram, eye], axis=1)
    width = 2 * size
    count = size // 8
    parts = [wide[8 * b : 8 * b + 8, :] for b in range(count)]
    sub = lax.broadcasted_iota(jnp.int32, (8, width), 0)

    def lift(value, s):
        return jnp.broadcast_to(value[s : s + 1, :], (8, width))

    scales = []
    for b in range(count):
        columns = {
            i: [
                jnp.broadcast_to(parts[i][:, 8 * b + j : 8 * b + j + 1], (8, width))
                for j in range(8)
            ]
            for i in range(b, count)
        }
        lead = columns[b]
        for s in range(8):
            pivot = lift(lead[s], s)
            inverse = 1.0 / pivot
            if s == 0:
                scale = inverse
            else:
                scale = jnp.where(sub == s, inverse, scale)
            factors = {i: columns[i][s] * inverse for i in range(b, count)}
            factors[b] = jnp.where(sub > s, factors[b], 0.0)
            for j in range(s + 1, 8):
                top = lift(lead[j], s)
                for i in range(b, count):
                    columns[i][j] = columns[i][j] - factors[i] * top
            top = lift(parts[b], s)
            for i in range(b, count):
                parts[i] = parts[i] - factors[i] * top
        scales.append(scale)
    return jnp.concatenate(
        [(parts[b] * jnp.sqrt(scales[b]))[:, size:] for b in range(count)], axis=0
    )


def kernel(
    row_count, col_count, atom_total,
    v_hbm, off_hbm, cnt_hbm, lab_hbm, cos_hbm, dist_hbm, out_ref,
    v_ref, off_ref, cnt_ref, lab_ref, cos_ref, dist_ref,
    key, hop, site, w_high, w_low, ext, ext_2, mid, fin, halo, gram, gx, gsum, rs, slab, zs, tot, gat, swap,
    send, recv, load,
):
    vector_count, local = v_ref.shape
    tiles = local // TILE
    planes = row_count // 4
    r, c = lax.axis_index("rows"), lax.axis_index("cols")
    place = r * col_count + c
    total = row_count * col_count
    ahead = lax.rem(place + 1, total)
    behind = lax.rem(place + total - 1, total)
    right = (ahead // col_count, lax.rem(ahead, col_count))
    left = (behind // col_count, lax.rem(behind, col_count))
    bit0, bit1 = lax.rem(r, 2), lax.rem(r // 2, 2)
    z = r // 4
    mine = lax.rem(r, 4)

    loads = [
        pltpu.make_async_copy(source, target, load.at[n])
        for n, (source, target) in enumerate((
            (off_hbm, off_ref), (cos_hbm, cos_ref), (dist_hbm, dist_ref),
            (cnt_hbm, cnt_ref), (lab_hbm, lab_ref), (v_hbm, v_ref),
        ))
    ]
    for copy in loads:
        copy.start()

    group = []
    for j in range(1, 4):
        p0 = 1 - bit0 if j & 1 else bit0
        p1 = 1 - bit1 if j & 2 else bit1
        group.append(((4 * z + 2 * p1 + p0, c), p0 + 2 * p1))
    peers = [(4 * lax.rem(z + d, planes) + lax.rem(r, 4), c) for d in range(1, planes)]
    partner = (r, 1 - c)

    barrier = pltpu.get_barrier_semaphore()
    greeted = [left, right, partner] + [g[0] for g in group] + peers
    for device in greeted:
        pl.semaphore_signal(barrier, inc=1, device_id=device, device_id_type=MESH)

    def remote(slot, source, target, device):
        return pltpu.make_async_remote_copy(
            src_ref=source, dst_ref=target, send_sem=send.at[slot], recv_sem=recv.at[slot],
            device_id=device, device_id_type=MESH,
        )

    def edges(source, first):
        low = source.at[:, pl.ds(local - REACH, REACH)]
        high = source.at[:, pl.ds(0, REACH)]
        to_right = remote(first, low, halo.at[first], right)
        to_left = remote(first + 1, high, halo.at[first + 1], left)
        to_right.start()
        to_left.start()
        return to_right, to_left

    for copy in loads[:5]:
        copy.wait()
    lane = lax.broadcasted_iota(jnp.int32, (1, local), 1)
    keys_all, hops_all = merged(
        off_ref[...] + (lax.rem(lane, HALF) + REACH),
        hop_table_2(cos_ref[...], dist_ref[...], cnt_ref[...]),
    )
    key[...] = keys_all
    hop[...] = hops_all
    lab = lab_ref[...]
    signs = (2 * lab - 1).astype(jnp.float32)
    site[...] = SITE_MASS * signs[0:1, :] + LAYER_BIAS * signs[1:2, :]

    pl.semaphore_wait(barrier, len(greeted))
    halo_a = edges(v_hbm, 0)

    def put_ext(target, value, first, width):
        high, low = split_2(value)
        target[0:vector_count, first : first + width] = high
        target[vector_count : 2 * vector_count, first : first + width] = low

    slots = off_ref.shape[0]
    chunk = 64
    row16 = lax.broadcasted_iota(jnp.int32, (16, HALF), 0)

    def build(t):
        for half in range(2):
            lanes = pl.ds(pl.multiple_of(t * TILE + half * HALF, HALF), HALF)
            span = pl.ds(half * HALF, HALF)
            keys = key[:, lanes]
            hops = hop[:, lanes]
            keys = [
                jnp.broadcast_to(keys[k : k + 1, :], (16, HALF)).astype(jnp.int16)
                for k in range(slots)
            ]
            hops = [
                split_2(jnp.broadcast_to(hops[k : k + 1, :], (16, HALF))) for k in range(slots)
            ]

            def rows(q, inner):
                for piece in range(chunk // 16):
                    index = (row16 + (q * chunk + piece * 16)).astype(jnp.int16)
                    high = low = jnp.zeros((16, HALF), jnp.bfloat16)
                    for k in range(slots):
                        here = keys[k] == index
                        high = jnp.where(here, hops[k][0], high)
                        low = jnp.where(here, hops[k][1], low)
                    first = pl.multiple_of(q * chunk + piece * 16 + half * HALF, 16)
                    w_high[t, pl.ds(first, 16), span] = high
                    w_low[t, pl.ds(first, 16), span] = low
                return inner

            lax.fori_loop(0, BAND // chunk, rows, 0)
            blank = jnp.zeros((HALF, HALF), jnp.bfloat16)
            edge = pl.ds(BAND if half == 0 else 0, HALF)
            w_high[t, edge, pl.ds(half * HALF, HALF)] = blank
            w_low[t, edge, pl.ds(half * HALF, HALF)] = blank

    def build_all(n, carry):
        build(n)
        return carry

    lax.fori_loop(0, tiles, build_all, 0)

    def apply(t, ext, source, target):
        lanes = slice(t * TILE, (t + 1) * TILE)
        span = slice(t * TILE, t * TILE + SPAN)
        both = dot_nn(ext[:, span], w_high[t])
        value = both[0:vector_count] + both[vector_count:]
        value = value + dot_nn(ext[0:vector_count, span], w_low[t])
        target[:, lanes] = value + site[:, lanes] * source[:, lanes]

    last = tiles - 1
    loads[5].wait()
    put_ext(ext, v_ref[...], REACH, local)
    for t in range(1, last):
        apply(t, ext, v_ref, mid)
    halo_a[0].wait_recv()
    halo_a[1].wait_recv()
    put_ext(ext, halo[0], 0, REACH)
    put_ext(ext, halo[1], REACH + local, REACH)
    apply(0, ext, v_ref, mid)
    apply(last, ext, v_ref, mid)
    halo_b = edges(mid, 2)
    put_ext(ext_2, mid[...], REACH, local)

    base = 20
    swaps = []

    def send_tile(t):
        pair = []
        for b in range(2):
            piece = (pl.ds(b * BLOCK, BLOCK), pl.ds(t * TILE, TILE))
            pair.append(
                remote(base + 2 * t + b, fin.at[piece], swap.at[piece], partner)
            )
        pair[0].start()

        @pl.when(c == 0)
        def _():
            pair[1].start()

        swaps.append((t, pair))

    for t in range(1, last):
        apply(t, ext_2, mid, fin)
    halo_b[0].wait_recv()
    halo_b[1].wait_recv()
    put_ext(ext_2, halo[2], 0, REACH)
    put_ext(ext_2, halo[3], REACH + local, REACH)
    apply(0, ext_2, mid, fin)
    apply(last, ext_2, mid, fin)

    high, low = split_2(fin[...])
    lead = jnp.concatenate([high[0:BLOCK], low[0:BLOCK]], axis=0)
    pair = dot_nt(lead, jnp.concatenate([high, low], axis=0))
    part = pair[0:BLOCK, 0:vector_count] + (
        pair[BLOCK:, 0:vector_count] + pair[0:BLOCK, vector_count:]
    )
    part = part * (1.0 / atom_total)
    for b in range(4):
        gram[b] = part[16 * b : 16 * b + 16, :]

    couple = remote(10, gram, gx, partner)
    couple.start()
    for t in (*range(1, last), 0, last):
        send_tile(t)
    couple.wait_recv()
    gsum[...] = gram[...] + gx[...]

    scatter = []
    for j in range(3):
        device, index = group[j]
        copy = remote(4 + j, gsum.at[index], rs.at[j], device)
        copy.start()
        scatter.append(copy)

    value = gsum[mine]
    for j in range(3):
        scatter[j].wait_recv()
        value = value + rs[j]
    slab[...] = value
    across = []
    first = base + 2 * tiles
    for d in range(len(peers)):
        copy = remote(first + d, slab, zs.at[d], peers[d])
        copy.start()
        across.append(copy)
    for d in range(len(peers)):
        across[d].wait_recv()
        value = value + zs[d]
    tot[...] = value
    gather = []
    for j in range(3):
        copy = remote(7 + j, tot, gat.at[mine], group[j][0])
        copy.start()
        gather.append(copy)
    gat[mine] = value
    for j in range(3):
        gather[j].wait_recv()

    highest = lax.Precision.HIGHEST
    full = jnp.concatenate([gat[b] for b in range(4)], axis=0)
    inverse = inverse_factor(full[:, 0:BLOCK])
    coupling = jnp.dot(
        inverse, full[:, BLOCK:], precision=highest, preferred_element_type=jnp.float32
    )
    update = lax.dot_general(
        coupling, inverse, (((0,), (0,)), ((), ())), precision=highest,
        preferred_element_type=jnp.float32,
    )
    owner = c == 0
    factor_high, factor_low = split_2(jnp.where(owner, inverse, -update))
    factor = jnp.concatenate([factor_high, factor_low], axis=0)

    def result(lead_high, lead_low, own):
        both = dot_nn(factor, lead_high)
        value = both[0:BLOCK] + both[BLOCK:] + dot_nn(factor_high, lead_low)
        return value + jnp.where(owner, 0.0, own)

    own = result(high[0:BLOCK], low[0:BLOCK], fin[BLOCK:, :])
    out_ref[:, pl.ds(pl.multiple_of(c * local, local), local)] = own

    there = pl.multiple_of((1 - c) * local, local)
    for t, pair in swaps:
        pair[0].wait_recv()

        @pl.when(c == 1)
        def _():
            pair[1].wait_recv()

        lanes = slice(t * TILE, (t + 1) * TILE)
        other_high, other_low = split_2(swap[0:BLOCK, lanes])
        theirs = result(other_high, other_low, swap[BLOCK:, lanes])
        out_ref[:, pl.ds(pl.multiple_of(there + t * TILE, TILE), TILE)] = theirs

    for copy in (*halo_a, *halo_b, couple, *scatter, *across, *gather):
        copy.wait_send()
    for t, pair in swaps:
        pair[0].wait_send()

        @pl.when(c == 0)
        def _():
            pair[1].wait_send()


def merged(keys, values):
    count = keys.shape[0]
    row = lax.broadcasted_iota(jnp.int32, keys.shape, 0)
    repeated = jnp.zeros(keys.shape, jnp.int32)
    total = values
    for shift in range(1, count):
        near = jnp.concatenate([keys[count - shift :], keys[: count - shift]], axis=0)
        value = jnp.concatenate([values[count - shift :], values[: count - shift]], axis=0)
        same = near == keys
        later = row < shift
        total = total + jnp.where(same & later, value, 0.0)
        repeated = jnp.where(same & ~later, 1, repeated)
    return jnp.where(repeated == 1, -1, keys), total


def hop_table_2(cosines, distances, counts):
    square = cosines * cosines
    bond_value = PI_BOND * jnp.exp(-(distances - 1.0) / DECAY_LENGTH) * (1.0 - square)
    bond_value = bond_value + SIGMA_BOND * jnp.exp(-(distances - LAYER_GAP) / DECAY_LENGTH) * square
    slot_index = lax.broadcasted_iota(jnp.int32, cosines.shape, 0)
    return jnp.where(slot_index < counts, bond_value, jnp.zeros_like(bond_value))


def fused(row_count, col_count, vectors, offsets, counts, labels, cosines, distances):
    vector_count, local = vectors.shape
    slots = offsets.shape[0]
    tiles = local // TILE
    planes = row_count // 4
    f32, bf16 = jnp.float32, jnp.bfloat16
    vmem = pl.BlockSpec(memory_space=pltpu.VMEM)
    peers = planes - 1
    semaphores = 20 + 2 * tiles + peers
    return pl.pallas_call(
        functools.partial(kernel, row_count, col_count, local * row_count * col_count),
        out_shape=pltpu.VMEM((BLOCK, local * col_count), f32),
        in_specs=[pl.BlockSpec(memory_space=pltpu.HBM)] * 6,
        out_specs=vmem,
        scratch_shapes=[
            pltpu.VMEM((vector_count, local), f32),
            pltpu.VMEM((slots, local), jnp.int32),
            pltpu.VMEM((1, local), jnp.int32),
            pltpu.VMEM((2, local), jnp.int32),
            pltpu.VMEM((slots, local), f32),
            pltpu.VMEM((slots, local), f32),
            pltpu.VMEM((slots, local), jnp.int32),
            pltpu.VMEM((slots, local), f32),
            pltpu.VMEM((1, local), f32),
            pltpu.VMEM((tiles, SPAN, TILE), bf16),
            pltpu.VMEM((tiles, SPAN, TILE), bf16),
            pltpu.VMEM((2 * vector_count, local + 2 * REACH), bf16),
            pltpu.VMEM((2 * vector_count, local + 2 * REACH), bf16),
            pltpu.VMEM((vector_count, local), f32),
            pltpu.VMEM((vector_count, local), f32),
            pltpu.VMEM((4, vector_count, REACH), f32),
            pltpu.VMEM((4, 16, vector_count), f32),
            pltpu.VMEM((4, 16, vector_count), f32),
            pltpu.VMEM((4, 16, vector_count), f32),
            pltpu.VMEM((3, 16, vector_count), f32),
            pltpu.VMEM((16, vector_count), f32),
            pltpu.VMEM((peers, 16, vector_count), f32),
            pltpu.VMEM((16, vector_count), f32),
            pltpu.VMEM((4, 16, vector_count), f32),
            pltpu.VMEM((vector_count, local), f32),
            pltpu.SemaphoreType.DMA((semaphores,)),
            pltpu.SemaphoreType.DMA((semaphores,)),
            pltpu.SemaphoreType.DMA((6,)),
        ],
        compiler_params=pltpu.CompilerParams(
            collective_id=0, has_side_effects=True, vmem_limit_bytes=60 * 1024 * 1024
        ),
    )(vectors, offsets, counts.reshape(1, local), labels, cosines, distances)


def fits(row_count, col_count, vectors):
    vector_count, local = vectors.shape
    return (
        col_count == 2
        and row_count in (8, 12, 16, 20, 24, 28, 32)
        and vector_count == 2 * BLOCK
        and local % TILE == 0
        and local >= 2 * TILE
    )


def on_slice(row_count, col_count, *arguments):
    if fits(row_count, col_count, arguments[0]):
        return fused(row_count, col_count, *arguments)
    return on_device(*arguments)


def solution(mesh):
    placed = (
        P(None, ("rows", "cols")),
        P(None, ("rows", "cols")),
        P(("rows", "cols")),
        P(None, ("rows", "cols")),
        P(None, ("rows", "cols")),
        P(None, ("rows", "cols")),
    )
    return jax.shard_map(
        functools.partial(on_slice, mesh.shape["rows"], mesh.shape["cols"]),
        mesh=mesh, in_specs=placed, out_specs=P("cols", "rows"), check_vma=False
    )
```

```python
import functools

import jax
import jax.numpy as jnp
from jax import lax
from jax.experimental import pallas as pl
from jax.experimental.pallas import tpu as pltpu
from jax.sharding import PartitionSpec as P

REACH = 256


PI_BOND = -1.0
SIGMA_BOND = 0.178
DECAY_LENGTH = 0.319
LAYER_GAP = 2.36
SITE_MASS = 0.4
LAYER_BIAS = 0.25


def extended_2(block, sides, width):
    for axis, dim in sides:
        count = lax.axis_size(axis)
        forward = [(i, i + 1) for i in range(count - 1)]
        forward.append((count - 1, 0))
        backward = [(target, source) for source, target in forward]
        low = lax.ppermute(
            lax.slice_in_dim(block, block.shape[dim] - width, None, axis=dim), axis, forward
        )
        high = lax.ppermute(lax.slice_in_dim(block, 0, width, axis=dim), axis, backward)
        block = jnp.concatenate([low, block, high], axis=dim)
    return block


def spread(value, axis, source):
    kept = jnp.where(lax.axis_index(axis) == source, value, 0).astype(value.dtype)
    return lax.psum(kept, axis)


def hop_table(cosines, distances, counts):
    square = cosines * cosines
    bond_value = PI_BOND * jnp.exp(-(distances - 1.0) / DECAY_LENGTH) * (1.0 - square)
    bond_value = bond_value + SIGMA_BOND * jnp.exp(-(distances - LAYER_GAP) / DECAY_LENGTH) * square
    slot_index = lax.broadcasted_iota(jnp.int32, cosines.shape, 0)
    return jnp.where(slot_index < counts[None, :], bond_value, jnp.zeros_like(bond_value))


def onsite_of(labels):
    sublattice = (2 * labels[0] - 1).astype(jnp.float32)
    layer_sign = (2 * labels[1] - 1).astype(jnp.float32)
    return SITE_MASS * sublattice + LAYER_BIAS * layer_sign


def apply_local(extended, hopping, offsets, onsite):
    atom_count = hopping.shape[1]
    middle = extended[:, REACH : REACH + atom_count]
    column = jnp.arange(atom_count, dtype=jnp.int32) + REACH

    def advance(slot_index, running):
        target = column + offsets[slot_index]
        return running + hopping[slot_index][None, :] * jnp.take(extended, target, axis=1)

    return lax.fori_loop(0, hopping.shape[0], advance, onsite[None, :] * middle)


def regroup(source):
    return lax.all_to_all(source, "cols", split_axis=0, concat_axis=1, tiled=True)


def on_device(vectors, offsets, counts, labels, cosines, distances):
    highest = lax.Precision.HIGHEST
    hopping = hop_table(cosines, distances, counts)
    onsite = onsite_of(labels)
    applied = vectors
    for repeat in range(2):
        extended = extended_2(applied, ((("rows", "cols"), 1),), REACH)
        applied = apply_local(extended, hopping, offsets, onsite)
    local_block = regroup(applied)
    atom_total = local_block.shape[1] * lax.axis_size("rows")
    step_count = min(3, lax.axis_size("cols") - 1)
    column_index = lax.axis_index("cols")
    for step_index in range(step_count):
        gram_matrix = (
            lax.psum(jnp.dot(local_block, local_block.T, precision=highest), "rows") / atom_total
        )
        factor = jnp.linalg.cholesky(gram_matrix)
        candidate = jax.scipy.linalg.solve_triangular(factor, local_block, lower=True)
        leader = spread(candidate, "cols", step_index)
        coupling = lax.psum(jnp.dot(leader, local_block.T, precision=highest), "rows") / atom_total
        reduced = local_block - jnp.dot(coupling.T, leader, precision=highest)
        local_block = jnp.where(
            column_index > step_index,
            reduced,
            jnp.where(column_index == step_index, leader, local_block),
        )
    return local_block


BLOCK = 64
TILE = 256
SPAN = TILE + 2 * REACH
HALF = 128
BAND = HALF + 2 * REACH
MESH = pl.DeviceIdType.MESH


def split_2(value):
    high = value.astype(jnp.bfloat16)
    low = (value - high.astype(jnp.float32)).astype(jnp.bfloat16)
    return high, low


def dot_nn(left, right):
    return lax.dot_general(
        left, right, (((1,), (0,)), ((), ())), preferred_element_type=jnp.float32
    )


def dot_nt(left, right):
    return lax.dot_general(
        left, right, (((1,), (1,)), ((), ())), preferred_element_type=jnp.float32
    )


def inverse_factor(gram):
    size = gram.shape[0]
    rows = lax.broadcasted_iota(jnp.int32, (size, size), 0)
    lanes = lax.broadcasted_iota(jnp.int32, (size, size), 1)
    eye = jnp.where(rows == lanes, 1.0, 0.0).astype(jnp.float32)
    wide = jnp.concatenate([gram, eye], axis=1)
    width = 2 * size
    count = size // 8
    parts = [wide[8 * b : 8 * b + 8, :] for b in range(count)]
    sub = lax.broadcasted_iota(jnp.int32, (8, width), 0)

    def lift(value, s):
        return jnp.broadcast_to(value[s : s + 1, :], (8, width))

    scales = []
    for b in range(count):
        columns = {
            i: [
                jnp.broadcast_to(parts[i][:, 8 * b + j : 8 * b + j + 1], (8, width))
                for j in range(8)
            ]
            for i in range(b, count)
        }
        lead = columns[b]
        for s in range(8):
            pivot = lift(lead[s], s)
            rough = pl.reciprocal(pivot, approx=True)
            inverse = rough * (2.0 - pivot * rough)
            if s == 0:
                scale = inverse
            else:
                scale = jnp.where(sub == s, inverse, scale)
            factors = {i: columns[i][s] * inverse for i in range(b, count)}
            factors[b] = jnp.where(sub > s, factors[b], 0.0)
            for j in range(s + 1, 8):
                top = lift(lead[j], s)
                for i in range(b, count):
                    columns[i][j] = columns[i][j] - factors[i] * top
            top = lift(parts[b], s)
            for i in range(b, count):
                parts[i] = parts[i] - factors[i] * top
        scales.append(scale)
    return jnp.concatenate(
        [(parts[b] * jnp.sqrt(scales[b]))[:, size:] for b in range(count)], axis=0
    )


def kernel(
    row_count, col_count, atom_total,
    v_hbm, off_hbm, cnt_hbm, lab_hbm, cos_hbm, dist_hbm, out_ref,
    v_ref, off_ref, cnt_ref, lab_ref, cos_ref, dist_ref,
    key, hop, site, w_high, w_low, ext, ext_2, mid, fin, halo, gram, rs, slab, zs, tot, gat, swap,
    send, recv, load,
):
    vector_count, local = v_ref.shape
    tiles = local // TILE
    planes = row_count // 4
    r, c = lax.axis_index("rows"), lax.axis_index("cols")
    place = r * col_count + c
    total = row_count * col_count
    ahead = lax.rem(place + 1, total)
    behind = lax.rem(place + total - 1, total)
    right = (ahead // col_count, lax.rem(ahead, col_count))
    left = (behind // col_count, lax.rem(behind, col_count))
    bit0, bit1 = lax.rem(r, 2), lax.rem(r // 2, 2)
    z = r // 4
    mine = lax.rem(r, 4)

    loads = [
        pltpu.make_async_copy(source, target, load.at[n])
        for n, (source, target) in enumerate((
            (off_hbm, off_ref), (cos_hbm, cos_ref), (dist_hbm, dist_ref),
            (cnt_hbm, cnt_ref), (lab_hbm, lab_ref), (v_hbm, v_ref),
        ))
    ]
    for copy in loads:
        copy.start()

    group = []
    for j in range(1, 4):
        p0 = 1 - bit0 if j & 1 else bit0
        p1 = 1 - bit1 if j & 2 else bit1
        group.append(((4 * z + 2 * p1 + p0, c), p0 + 2 * p1))
    peers = [
        (4 * lax.rem(z + d, planes) + lax.rem(r, 4), 1 - c if dx else c)
        for dx in range(2)
        for d in range(planes)
        if dx or d
    ]
    partner = (r, 1 - c)

    barrier = pltpu.get_barrier_semaphore()
    greeted = [left, right] + [g[0] for g in group] + peers
    for device in greeted:
        pl.semaphore_signal(barrier, inc=1, device_id=device, device_id_type=MESH)

    def remote(slot, source, target, device):
        return pltpu.make_async_remote_copy(
            src_ref=source, dst_ref=target, send_sem=send.at[slot], recv_sem=recv.at[slot],
            device_id=device, device_id_type=MESH,
        )

    def edges(source, first):
        low = source.at[:, pl.ds(local - REACH, REACH)]
        high = source.at[:, pl.ds(0, REACH)]
        to_right = remote(first, low, halo.at[first], right)
        to_left = remote(first + 1, high, halo.at[first + 1], left)
        to_right.start()
        to_left.start()
        return to_right, to_left

    for copy in loads[:5]:
        copy.wait()
    lane = lax.broadcasted_iota(jnp.int32, (1, local), 1)
    keys_all, hops_all = merged(
        off_ref[...] + (lax.rem(lane, HALF) + REACH),
        hop_table_2(cos_ref[...], dist_ref[...], cnt_ref[...]),
    )
    key[...] = keys_all
    hop[...] = hops_all
    lab = lab_ref[...]
    signs = (2 * lab - 1).astype(jnp.float32)
    site[...] = SITE_MASS * signs[0:1, :] + LAYER_BIAS * signs[1:2, :]

    pl.semaphore_wait(barrier, len(greeted))
    halo_a = edges(v_hbm, 0)

    def put_ext(target, value, first, width):
        high, low = split_2(value)
        target[0:vector_count, first : first + width] = high
        target[vector_count : 2 * vector_count, first : first + width] = low

    slots = off_ref.shape[0]
    chunk = 64
    row16 = lax.broadcasted_iota(jnp.int32, (16, HALF), 0)

    def build(t):
        for half in range(2):
            lanes = pl.ds(pl.multiple_of(t * TILE + half * HALF, HALF), HALF)
            span = pl.ds(half * HALF, HALF)
            keys = key[:, lanes]
            hops = hop[:, lanes]
            keys = [
                jnp.broadcast_to(keys[k : k + 1, :], (16, HALF)).astype(jnp.int16)
                for k in range(slots)
            ]
            hops = [
                split_2(jnp.broadcast_to(hops[k : k + 1, :], (16, HALF))) for k in range(slots)
            ]

            def rows(q, inner):
                for piece in range(chunk // 16):
                    index = (row16 + (q * chunk + piece * 16)).astype(jnp.int16)
                    high = low = jnp.zeros((16, HALF), jnp.bfloat16)
                    for k in range(slots):
                        here = keys[k] == index
                        high = jnp.where(here, hops[k][0], high)
                        low = jnp.where(here, hops[k][1], low)
                    first = pl.multiple_of(q * chunk + piece * 16 + half * HALF, 16)
                    w_high[t, pl.ds(first, 16), span] = high
                    w_low[t, pl.ds(first, 16), span] = low
                return inner

            lax.fori_loop(0, BAND // chunk, rows, 0)
            blank = jnp.zeros((HALF, HALF), jnp.bfloat16)
            edge = pl.ds(BAND if half == 0 else 0, HALF)
            w_high[t, edge, pl.ds(half * HALF, HALF)] = blank
            w_low[t, edge, pl.ds(half * HALF, HALF)] = blank

    def build_all(n, carry):
        build(n)
        return carry

    lax.fori_loop(0, tiles, build_all, 0)

    def apply(t, ext, source, target):
        lanes = slice(t * TILE, (t + 1) * TILE)
        span = slice(t * TILE, t * TILE + SPAN)
        both = dot_nn(ext[:, span], w_high[t])
        value = both[0:vector_count] + both[vector_count:]
        value = value + dot_nn(ext[0:vector_count, span], w_low[t])
        target[:, lanes] = value + site[:, lanes] * source[:, lanes]

    last = tiles - 1
    loads[5].wait()
    put_ext(ext, v_ref[...], REACH, local)
    for t in range(1, last):
        apply(t, ext, v_ref, mid)
    halo_a[0].wait_recv()
    halo_a[1].wait_recv()
    put_ext(ext, halo[0], 0, REACH)
    put_ext(ext, halo[1], REACH + local, REACH)
    apply(0, ext, v_ref, mid)
    apply(last, ext, v_ref, mid)
    halo_b = edges(mid, 2)
    put_ext(ext_2, mid[...], REACH, local)

    base = 20
    swaps = []

    def send_tile(t):
        pair = []
        for b in range(2):
            piece = (pl.ds(b * BLOCK, BLOCK), pl.ds(t * TILE, TILE))
            pair.append(
                remote(base + 2 * t + b, fin.at[piece], swap.at[piece], partner)
            )
        pair[0].start()

        @pl.when(c == 0)
        def _():
            pair[1].start()

        swaps.append((t, pair))

    for t in range(1, last):
        apply(t, ext_2, mid, fin)
    halo_b[0].wait_recv()
    halo_b[1].wait_recv()
    put_ext(ext_2, halo[2], 0, REACH)
    put_ext(ext_2, halo[3], REACH + local, REACH)
    apply(0, ext_2, mid, fin)
    apply(last, ext_2, mid, fin)

    high, low = split_2(fin[...])
    lead = jnp.concatenate([high[0:BLOCK], low[0:BLOCK]], axis=0)
    pair = dot_nt(lead, jnp.concatenate([high, low], axis=0))
    part = pair[0:BLOCK, 0:vector_count] + (
        pair[BLOCK:, 0:vector_count] + pair[0:BLOCK, vector_count:]
    )
    part = part * (1.0 / atom_total)
    for b in range(4):
        gram[b] = part[16 * b : 16 * b + 16, :]

    scatter = []
    for j in range(3):
        device, index = group[j]
        copy = remote(4 + j, gram.at[index], rs.at[j], device)
        copy.start()
        scatter.append(copy)

    value = gram[mine]
    for j in range(3):
        scatter[j].wait_recv()
        value = value + rs[j]
    slab[...] = value
    across = []
    first = base + 2 * tiles
    for d in range(len(peers)):
        copy = remote(first + d, slab, zs.at[d], peers[d])
        copy.start()
        across.append(copy)
    for t in (*range(1, last), 0, last):
        send_tile(t)
    for d in range(len(peers)):
        across[d].wait_recv()
        value = value + zs[d]
    tot[...] = value
    gather = []
    for j in range(3):
        copy = remote(7 + j, tot, gat.at[mine], group[j][0])
        copy.start()
        gather.append(copy)
    gat[mine] = value
    for j in range(3):
        gather[j].wait_recv()

    highest = lax.Precision.HIGHEST
    full = jnp.concatenate([gat[b] for b in range(4)], axis=0)
    inverse = inverse_factor(full[:, 0:BLOCK])
    coupling = jnp.dot(
        inverse, full[:, BLOCK:], precision=highest, preferred_element_type=jnp.float32
    )
    update = lax.dot_general(
        coupling, inverse, (((0,), (0,)), ((), ())), precision=highest,
        preferred_element_type=jnp.float32,
    )
    owner = c == 0
    factor_high, factor_low = split_2(jnp.where(owner, inverse, -update))
    factor = jnp.concatenate([factor_high, factor_low], axis=0)

    def result(lead_high, lead_low, own):
        both = dot_nn(factor, lead_high)
        value = both[0:BLOCK] + both[BLOCK:] + dot_nn(factor_high, lead_low)
        return value + jnp.where(owner, 0.0, own)

    own = result(high[0:BLOCK], low[0:BLOCK], fin[BLOCK:, :])
    out_ref[:, pl.ds(pl.multiple_of(c * local, local), local)] = own

    there = pl.multiple_of((1 - c) * local, local)
    for t, pair in swaps:
        pair[0].wait_recv()

        @pl.when(c == 1)
        def _():
            pair[1].wait_recv()

        lanes = slice(t * TILE, (t + 1) * TILE)
        other_high, other_low = split_2(swap[0:BLOCK, lanes])
        theirs = result(other_high, other_low, swap[BLOCK:, lanes])
        out_ref[:, pl.ds(pl.multiple_of(there + t * TILE, TILE), TILE)] = theirs

    for copy in (*halo_a, *halo_b, *scatter, *across, *gather):
        copy.wait_send()
    for t, pair in swaps:
        pair[0].wait_send()

        @pl.when(c == 0)
        def _():
            pair[1].wait_send()


def merged(keys, values):
    count = keys.shape[0]
    row = lax.broadcasted_iota(jnp.int32, keys.shape, 0)
    repeated = jnp.zeros(keys.shape, jnp.int32)
    total = values
    for shift in range(1, count):
        near = jnp.concatenate([keys[count - shift :], keys[: count - shift]], axis=0)
        value = jnp.concatenate([values[count - shift :], values[: count - shift]], axis=0)
        same = near == keys
        later = row < shift
        total = total + jnp.where(same & later, value, 0.0)
        repeated = jnp.where(same & ~later, 1, repeated)
    return jnp.where(repeated == 1, -1, keys), total


def hop_table_2(cosines, distances, counts):
    square = cosines * cosines
    bond_value = PI_BOND * jnp.exp(-(distances - 1.0) / DECAY_LENGTH) * (1.0 - square)
    bond_value = bond_value + SIGMA_BOND * jnp.exp(-(distances - LAYER_GAP) / DECAY_LENGTH) * square
    slot_index = lax.broadcasted_iota(jnp.int32, cosines.shape, 0)
    return jnp.where(slot_index < counts, bond_value, jnp.zeros_like(bond_value))


def fused(row_count, col_count, vectors, offsets, counts, labels, cosines, distances):
    vector_count, local = vectors.shape
    slots = offsets.shape[0]
    tiles = local // TILE
    planes = row_count // 4
    f32, bf16 = jnp.float32, jnp.bfloat16
    vmem = pl.BlockSpec(memory_space=pltpu.VMEM)
    peers = 2 * planes - 1
    semaphores = 20 + 2 * tiles + peers
    return pl.pallas_call(
        functools.partial(kernel, row_count, col_count, local * row_count * col_count),
        out_shape=pltpu.VMEM((BLOCK, local * col_count), f32),
        in_specs=[pl.BlockSpec(memory_space=pltpu.HBM)] * 6,
        out_specs=vmem,
        scratch_shapes=[
            pltpu.VMEM((vector_count, local), f32),
            pltpu.VMEM((slots, local), jnp.int32),
            pltpu.VMEM((1, local), jnp.int32),
            pltpu.VMEM((2, local), jnp.int32),
            pltpu.VMEM((slots, local), f32),
            pltpu.VMEM((slots, local), f32),
            pltpu.VMEM((slots, local), jnp.int32),
            pltpu.VMEM((slots, local), f32),
            pltpu.VMEM((1, local), f32),
            pltpu.VMEM((tiles, SPAN, TILE), bf16),
            pltpu.VMEM((tiles, SPAN, TILE), bf16),
            pltpu.VMEM((2 * vector_count, local + 2 * REACH), bf16),
            pltpu.VMEM((2 * vector_count, local + 2 * REACH), bf16),
            pltpu.VMEM((vector_count, local), f32),
            pltpu.VMEM((vector_count, local), f32),
            pltpu.VMEM((4, vector_count, REACH), f32),
            pltpu.VMEM((4, 16, vector_count), f32),
            pltpu.VMEM((3, 16, vector_count), f32),
            pltpu.VMEM((16, vector_count), f32),
            pltpu.VMEM((peers, 16, vector_count), f32),
            pltpu.VMEM((16, vector_count), f32),
            pltpu.VMEM((4, 16, vector_count), f32),
            pltpu.VMEM((vector_count, local), f32),
            pltpu.SemaphoreType.DMA((semaphores,)),
            pltpu.SemaphoreType.DMA((semaphores,)),
            pltpu.SemaphoreType.DMA((6,)),
        ],
        compiler_params=pltpu.CompilerParams(
            collective_id=0, has_side_effects=True, vmem_limit_bytes=60 * 1024 * 1024
        ),
    )(vectors, offsets, counts.reshape(1, local), labels, cosines, distances)


def fits(row_count, col_count, vectors):
    vector_count, local = vectors.shape
    return (
        col_count == 2
        and row_count in (8, 12, 16, 20, 24, 28, 32)
        and vector_count == 2 * BLOCK
        and local % TILE == 0
        and local >= 2 * TILE
    )


def on_slice(row_count, col_count, *arguments):
    if fits(row_count, col_count, arguments[0]):
        return fused(row_count, col_count, *arguments)
    return on_device(*arguments)


def solution(mesh):
    placed = (
        P(None, ("rows", "cols")),
        P(None, ("rows", "cols")),
        P(("rows", "cols")),
        P(None, ("rows", "cols")),
        P(None, ("rows", "cols")),
        P(None, ("rows", "cols")),
    )
    return jax.shard_map(
        functools.partial(on_slice, mesh.shape["rows"], mesh.shape["cols"]),
        mesh=mesh, in_specs=placed, out_specs=P("cols", "rows"), check_vma=False
    )
```
